32 devices in a mesh: rows: 4 (over y, x), cents: 8 (over z, core).
Axes of the slice: x: 2, y: 2, z: 4, core: 2. Of those that a mesh axis runs over, the one named last changes fastest.
Arguments:
- vectors: bfloat16 [2048, 1024], P(('rows', 'cents')), may hold values from -24 to 24, as said below
- centroids: bfloat16 [16384, 1024], P('cents'), may hold values from -0.1875 to 0.1875
Outputs:
- updated: bfloat16 [16384, 1024], P('cents', 'rows')
- masses: float32 [16384], P('cents')
The draws below stay inside these ranges and needn't reach their ends.
Inputs may be any that keep to these rules, and one draw needn't show every extreme that they name: `vectors`: entries are real-valued and of order one, with rows of differing scales.
All inputs are finite; a program needn't handle non-finite values.
Results may differ from the reference program's by a relative error of at most 0.015.
Values may be sent and summed in bfloat16 or wider, within the bound.
A program may use at most 128 MiB of HBM per device.

```python
import math
import jax
import jax.numpy as jnp
from jax import lax

EMBED = 1024
ROUNDS = 3
CENTROIDS = 16384
GROUP_ROWS = 512
BATCH = 2048
N_ROWS = 4


def draw_vectors(key, part):
    key = jax.random.fold_in(key, 11)
    first_key, second_key = jax.random.split(key)
    rise = 1.0 + 2.0 * jnp.arange(BATCH, dtype=jnp.float32) / max(BATCH - 1, 1)
    spread = jnp.exp(jax.random.uniform(second_key, (BATCH, 1), jnp.float32, math.log(0.5), math.log(2.0)))
    base = jnp.clip(jax.random.normal(first_key, (BATCH, EMBED), jnp.float32), -4.0, 4.0)
    return (base * spread * rise[:, None]).astype(jnp.bfloat16)


def shard_levels(rng, extent, pieces, low, top_value):
    level = 1.0
    for position, parts in pieces:
        draws = jax.random.uniform(jax.random.fold_in(jax.random.fold_in(rng, 6), position), (parts,), jnp.float32, low / len(pieces), top_value / len(pieces))
        level = level * jnp.repeat(jnp.exp(draws), extent[position] // parts).reshape((-1,) + (1,) * (len(extent) - 1 - position))
    return level


def scatter_about(stream_key, shape, width, bound, cuts=(), kind=jnp.bfloat16):
    loudness = shard_levels(stream_key, shape, cuts, -0.22, 0.18) if cuts else 1.0
    result = jax.random.normal(stream_key, shape, jnp.float32) * width * loudness
    return jnp.minimum(jnp.maximum(result, -bound), bound).astype(kind)


def setup_inputs(seed: int = 0) -> dict:
    streams_of = jax.random.split(jax.random.key(seed), 3)
    vectors = draw_vectors(jax.random.fold_in(streams_of[2], 71), 0)
    centroids = scatter_about(streams_of[1], (CENTROIDS, EMBED), EMBED ** -0.5, 0.1875, ((0, 8),))
    return dict(vectors=vectors, centroids=centroids)


SHARP = 0.75


def reference(vectors, centroids):
    logits = jnp.dot(vectors, centroids.T, preferred_element_type=jnp.float32)
    weights = jnp.exp(SHARP * logits)
    target = BATCH / CENTROIDS
    row_scale = jnp.ones((BATCH,), jnp.float32)
    col_scale = jnp.ones((CENTROIDS,), jnp.float32)
    for step in range(ROUNDS):
        colmass = jnp.dot(row_scale, weights, precision=lax.Precision.HIGHEST)
        col_scale = target / colmass
        rowmass = jnp.dot(weights, col_scale, precision=lax.Precision.HIGHEST)
        row_scale = 1.0 / rowmass
    masses = jnp.zeros((CENTROIDS,), jnp.float32)
    sums = jnp.zeros((CENTROIDS, EMBED), jnp.float32)
    for block in range(N_ROWS):
        first = block * GROUP_ROWS
        plan = weights[first:first + GROUP_ROWS] * row_scale[first:first + GROUP_ROWS, None] * col_scale[None, :]
        masses = masses + jnp.sum(plan, axis=0)
        plan_low = plan.astype(jnp.bfloat16)
        partial_value = lax.dot_general(plan_low, vectors[first:first + GROUP_ROWS], (((0,), (0,)), ((), ())), preferred_element_type=jnp.float32)
        partial_value = lax.optimization_barrier(partial_value.astype(jnp.bfloat16))
        sums = sums + partial_value.astype(jnp.float32)
    updated = 0.5 * centroids.astype(jnp.float32) + 0.5 * sums / masses[:, None]
    return updated.astype(jnp.bfloat16), masses
```

```python
import functools

import jax
import jax.numpy as jnp
from jax import lax
from jax.experimental import pallas as pl
from jax.experimental.pallas import tpu as pltpu

ROUNDS = 3
SHARP = 0.75
R = 4
LANES = 128
MESH = pl.DeviceIdType.MESH


def flip(a, d):
    out, bit = a, 1
    while bit <= d:
        if d & bit:
            out = out + bit - 2 * bit * lax.rem(lax.div(out, bit), 2)
        bit *= 2
    return out


def kernel(shards, target, vec, cent_hbm, out, mass_out, v, w, plan, cent, colb, massb, massrow, outbuf,
           part_a, part_b, box_a, box_b,
           gsend, grecv, asend, arecv, bsend, brecv, osend, orecv, msend, mrecv, lsem):
    r, c = lax.axis_index("rows"), lax.axis_index("cents")
    z, k = lax.div(c, 2), lax.rem(c, 2)
    depth = shards // 2
    rows = vec.shape[0]
    half = rows // 2
    mine = cent.shape[0]
    batch = v.shape[0]
    chunk = R * rows
    tiles = batch // LANES

    plane = [(q, s) for q in range(R) for s in range(2) if (q, s) != (0, 0)]

    def plane_dev(q, s):
        return (flip(r, q), flip(c, s))

    def z_dev(e):
        return (r, flip(z, e) * 2 + k)

    barrier = pltpu.get_barrier_semaphore()
    for q, s in plane:
        pl.semaphore_signal(barrier, inc=1, device_id=plane_dev(q, s), device_id_type=MESH)
    for e in range(1, depth):
        pl.semaphore_signal(barrier, inc=1, device_id=z_dev(e), device_id_type=MESH)
    cent_in = pltpu.make_async_copy(
        cent_hbm.at[pl.ds(pl.multiple_of(r * mine, mine), mine), :], cent, lsem.at[0])
    cent_in.start()
    pl.semaphore_wait(barrier, len(plane) + depth - 1)

    sent = []

    def piece(cc, rr, part):
        base = (cc * R + rr) * rows
        if part == 2:
            return v.at[pl.ds(pl.multiple_of(base, rows), rows), :]
        return v.at[pl.ds(pl.multiple_of(base + part * half, half), half), :]

    def gsem(cc, rr, part):
        return grecv.at[(cc * R + rr) * 2 + (0 if part == 2 else part)]

    def send(cc, rr, part, dev, src=None):
        copy = pltpu.make_async_remote_copy(
            src_ref=piece(cc, rr, part) if src is None else src,
            dst_ref=piece(cc, rr, part),
            send_sem=gsend.at[len(sent)],
            recv_sem=gsem(cc, rr, part),
            device_id=dev, device_id_type=MESH)
        copy.start()
        sent.append(copy)

    def arrive(cc, rr, part):
        ref = piece(cc, rr, part)
        pltpu.make_async_remote_copy(
            src_ref=ref, dst_ref=ref, send_sem=gsend.at[0], recv_sem=gsem(cc, rr, part),
            device_id=plane_dev(0, 1), device_id_type=MESH).wait_recv()

    east, north, other = plane_dev(1, 0), plane_dev(2, 0), plane_dev(0, 1)
    rx, ry, rd = flip(r, 1), flip(r, 2), flip(r, 3)

    def column(d):
        cc = flip(z, d) * 2 + k
        if d:
            arrive(cc, r, 2)
        src = None if d else vec
        send(cc, r, 2, east, src)
        send(cc, r, 2, north, src)
        send(cc, r, 2, other, src)

    def relay(d):
        cc = flip(z, d) * 2 + k
        arrive(cc, rx, 2)
        send(cc, rx, 0, north)
        send(cc, rx, 2, other)
        arrive(cc, ry, 2)
        send(cc, ry, 1, east)
        send(cc, ry, 2, other)

    def corner(d):
        cc = flip(z, d) * 2 + k
        arrive(cc, rd, 0)
        arrive(cc, rd, 1)
        send(cc, rd, 2, other)

    def weigh(cc):
        start = pl.multiple_of(cc * chunk, chunk)
        logits = lax.dot_general(
            cent[...], v[pl.ds(start, chunk), :], (((1,), (1,)), ((), ())),
            preferred_element_type=jnp.float32)
        w[:, pl.ds(start, chunk)] = jnp.exp(SHARP * logits)

    own = pltpu.make_async_copy(vec, piece(c, r, 2), lsem.at[1])
    own.start()
    if depth > 1:
        send(c, r, 2, z_dev(1), vec)
    column(0)
    for e in range(2, depth):
        send(c, r, 2, z_dev(e), vec)
    own.wait()
    cent_in.wait()
    for d in range(depth):
        relay(d)
        if d + 1 < depth:
            column(d + 1)
        corner(d)
        weigh(flip(z, d) * 2 + k)
        if d:
            cc = flip(z, d - 1) * 2 + 1 - k
            for rr in range(R):
                arrive(cc, rr, 2)
            weigh(cc)
    cc = flip(z, depth - 1) * 2 + 1 - k
    for rr in range(R):
        arrive(cc, rr, 2)
    weigh(cc)

    row_scale = jnp.ones((1, batch), jnp.float32)
    for step in range(ROUNDS):
        scales = [jnp.broadcast_to(row_scale[:, t * LANES:(t + 1) * LANES], (8, LANES)) for t in range(tiles)]

        def block(i, totals):
            at = pl.ds(pl.multiple_of(i * 8, 8), 8)
            terms = [w[at, t * LANES:(t + 1) * LANES] for t in range(tiles)]
            sums = [a * b for a, b in zip(terms, scales)]
            while len(sums) > 1:
                sums = [a + b for a, b in zip(sums[::2], sums[1::2])] + ([sums[-1]] if len(sums) % 2 else [])
            mass = jnp.sum(sums[0], axis=1, keepdims=True)
            col = jnp.broadcast_to(target / mass, (8, LANES))
            colb[at, :] = col
            return tuple(total + a * col for total, a in zip(totals, terms))

        totals = lax.fori_loop(
            0, mine // 8, block, tuple(jnp.zeros((8, LANES), jnp.float32) for _ in range(tiles)), unroll=4)
        for t in range(tiles):
            part_a[step, :, t * LANES:(t + 1) * LANES] = jnp.sum(totals[t], axis=0, keepdims=True)

        copies = []
        for j, (q, s) in enumerate(plane):
            copy = pltpu.make_async_remote_copy(
                src_ref=part_a.at[step], dst_ref=box_a.at[step, j], send_sem=asend.at[step, j],
                recv_sem=arecv.at[step, j], device_id=plane_dev(q, s), device_id_type=MESH)
            copy.start()
            copies.append(copy)
        total = part_a[step]
        for j, copy in enumerate(copies):
            copy.wait_recv()
            total = total + box_a[step, j]
        sent.extend(copies)
        part_b[step] = total
        copies = []
        for e in range(1, depth):
            copy = pltpu.make_async_remote_copy(
                src_ref=part_b.at[step], dst_ref=box_b.at[step, e], send_sem=bsend.at[step, e],
                recv_sem=brecv.at[step, e], device_id=z_dev(e), device_id_type=MESH)
            copy.start()
            copies.append(copy)
        for e, copy in enumerate(copies):
            copy.wait_recv()
            total = total + box_b[step, e + 1]
        sent.extend(copies)
        row_scale = 1.0 / total

    scales = [jnp.broadcast_to(row_scale[:, t * LANES:(t + 1) * LANES], (16, LANES)) for t in range(tiles)]

    def block(i, carry):
        at = pl.ds(pl.multiple_of(i * 16, 16), 16)
        col = colb[at, :]
        mass = jnp.zeros((16, LANES), jnp.float32)
        for t in range(tiles):
            term = w[at, t * LANES:(t + 1) * LANES] * scales[t] * col
            mass = mass + term
            plan[at, t * LANES:(t + 1) * LANES] = term.astype(jnp.bfloat16)
        massb[at, :] = jnp.broadcast_to(jnp.sum(mass, axis=1, keepdims=True), (16, LANES))
        return carry

    lax.fori_loop(0, mine // 16, block, 0, unroll=2)

    width = out.shape[1]
    results = []
    for q in (3, 1, 2, 0):
        peer = flip(r, q)
        cols = pl.ds(pl.multiple_of(peer * width, width), width)
        sums = jnp.dot(plan[...], v[:, cols], preferred_element_type=jnp.float32)
        mass = jnp.concatenate([massb[...]] * (width // LANES), axis=1)
        outbuf[q] = (0.5 * cent[:, cols].astype(jnp.float32) + 0.5 * sums / mass).astype(jnp.bfloat16)
        dst = out.at[pl.ds(pl.multiple_of(r * mine, mine), mine), :]
        if q:
            copy = pltpu.make_async_remote_copy(
                src_ref=outbuf.at[q], dst_ref=dst, send_sem=osend.at[q], recv_sem=orecv.at[q],
                device_id=(peer, c), device_id_type=MESH)
        else:
            copy = pltpu.make_async_copy(outbuf.at[q], dst, lsem.at[2])
        copy.start()
        results.append((q, copy))

    massrow[...] = jnp.transpose(massb[...], (1, 0))[:8, :]
    mdst = mass_out.at[pl.ds(pl.multiple_of(r * 8, 8), 8), :]
    mcopies = []
    for q in range(1, R):
        copy = pltpu.make_async_remote_copy(
            src_ref=massrow, dst_ref=mdst, send_sem=msend.at[q], recv_sem=mrecv.at[q],
            device_id=(flip(r, q), c), device_id_type=MESH)
        copy.start()
        mcopies.append(copy)
    local = pltpu.make_async_copy(massrow, mdst, lsem.at[3])
    local.start()

    for copy in sent:
        copy.wait_send()
    local.wait()
    for copy in mcopies:
        copy.wait()
    for q, copy in results:
        copy.wait()


def body(vectors, centroids, shards):
    rows, embed = vectors.shape
    batch = rows * R * shards
    held = centroids.shape[0]
    mine = held // R
    width = embed // R
    target = batch / (held * shards)
    depth = shards // 2
    f32, bf16 = jnp.float32, jnp.bfloat16
    dma = pltpu.SemaphoreType.DMA
    updated, masses = pl.pallas_call(
        functools.partial(kernel, shards, target),
        out_shape=(jax.ShapeDtypeStruct((held, width), bf16), jax.ShapeDtypeStruct((R * 8, mine), f32)),
        in_specs=[pl.BlockSpec(memory_space=pltpu.VMEM), pl.BlockSpec(memory_space=pl.ANY)],
        out_specs=(pl.BlockSpec(memory_space=pl.ANY), pl.BlockSpec(memory_space=pl.ANY)),
        scratch_shapes=[
            pltpu.VMEM((batch, embed), bf16),
            pltpu.VMEM((mine, batch), f32),
            pltpu.VMEM((mine, batch), bf16),
            pltpu.VMEM((mine, embed), bf16),
            pltpu.VMEM((mine, LANES), f32),
            pltpu.VMEM((mine, LANES), f32),
            pltpu.VMEM((8, mine), f32),
            pltpu.VMEM((R, mine, width), bf16),
            pltpu.VMEM((ROUNDS, 1, batch), f32),
            pltpu.VMEM((ROUNDS, 1, batch), f32),
            pltpu.VMEM((ROUNDS, 2 * R - 1, 1, batch), f32),
            pltpu.VMEM((ROUNDS, depth, 1, batch), f32),
            dma((depth * 9,)), dma((shards * R * 2,)),
            dma((ROUNDS, 2 * R)), dma((ROUNDS, 2 * R)),
            dma((ROUNDS, depth)), dma((ROUNDS, depth)),
            dma((R,)), dma((R,)), dma((R,)), dma((R,)), dma((4,)),
        ],
        compiler_params=pltpu.CompilerParams(
            collective_id=0, has_side_effects=True, vmem_limit_bytes=56 * 1024 * 1024),
        cost_estimate=pl.CostEstimate(
            flops=4 * mine * batch * embed, bytes_accessed=2 * mine * embed * 4, transcendentals=mine * batch),
    )(vectors, centroids)
    return updated, masses.reshape(R, 8, mine)[:, 0, :].reshape(held)


def solution(mesh):
    from jax.sharding import PartitionSpec as P
    return jax.shard_map(
        functools.partial(body, shards=mesh.shape["cents"]),
        mesh=mesh,
        in_specs=(P(("rows", "cents"), None), P("cents", None)),
        out_specs=(P("cents", "rows"), P("cents")),
        check_vma=False,
    )
```

```python
import functools

import jax
import jax.numpy as jnp
from jax import lax
from jax.experimental import pallas as pl
from jax.experimental.pallas import tpu as pltpu

ROUNDS = 3
SHARP = 0.75
R = 4
LANES = 128
MESH = pl.DeviceIdType.MESH


def flip(a, d):
    out, bit = a, 1
    while bit <= d:
        if d & bit:
            out = out + bit - 2 * bit * lax.rem(lax.div(out, bit), 2)
        bit *= 2
    return out


def kernel(shards, target, vec, cent_hbm, out, mass_out, v, w, plan, cent, colb, massb, massrow, outbuf,
           part_a, part_b, box_a, box_b,
           gsend, grecv, asend, arecv, bsend, brecv, osend, orecv, msend, mrecv, lsem):
    r, c = lax.axis_index("rows"), lax.axis_index("cents")
    z, k = lax.div(c, 2), lax.rem(c, 2)
    depth = shards // 2
    rows = vec.shape[0]
    half = rows // 2
    mine = cent.shape[0]
    batch = v.shape[0]
    chunk = R * rows
    tiles = batch // LANES

    plane = [(q, s) for q in range(R) for s in range(2) if (q, s) != (0, 0)]

    def plane_dev(q, s):
        return (flip(r, q), flip(c, s))

    def z_dev(e):
        return (r, flip(z, e) * 2 + k)

    barrier = pltpu.get_barrier_semaphore()
    for q, s in plane:
        pl.semaphore_signal(barrier, inc=1, device_id=plane_dev(q, s), device_id_type=MESH)
    for e in range(1, depth):
        pl.semaphore_signal(barrier, inc=1, device_id=z_dev(e), device_id_type=MESH)
    cent_in = pltpu.make_async_copy(
        cent_hbm.at[pl.ds(pl.multiple_of(r * mine, mine), mine), :], cent, lsem.at[0])
    cent_in.start()
    pl.semaphore_wait(barrier, len(plane) + depth - 1)

    sent = []

    def piece(cc, rr, part):
        base = (cc * R + rr) * rows
        if part == 2:
            return v.at[pl.ds(pl.multiple_of(base, rows), rows), :]
        return v.at[pl.ds(pl.multiple_of(base + part * half, half), half), :]

    def gsem(cc, rr, part):
        return grecv.at[(cc * R + rr) * 2 + (0 if part == 2 else part)]

    def send(cc, rr, part, dev, src=None):
        copy = pltpu.make_async_remote_copy(
            src_ref=piece(cc, rr, part) if src is None else src,
            dst_ref=piece(cc, rr, part),
            send_sem=gsend.at[len(sent)],
            recv_sem=gsem(cc, rr, part),
            device_id=dev, device_id_type=MESH)
        copy.start()
        sent.append(copy)

    def arrive(cc, rr, part):
        ref = piece(cc, rr, part)
        pltpu.make_async_remote_copy(
            src_ref=ref, dst_ref=ref, send_sem=gsend.at[0], recv_sem=gsem(cc, rr, part),
            device_id=plane_dev(0, 1), device_id_type=MESH).wait_recv()

    east, north, other = plane_dev(1, 0), plane_dev(2, 0), plane_dev(0, 1)
    rx, ry, rd = flip(r, 1), flip(r, 2), flip(r, 3)

    def column(d):
        cc = flip(z, d) * 2 + k
        if d:
            arrive(cc, r, 2)
        src = None if d else vec
        send(cc, r, 2, east, src)
        send(cc, r, 2, north, src)
        send(cc, r, 2, other, src)

    def relay(d):
        cc = flip(z, d) * 2 + k
        arrive(cc, rx, 2)
        send(cc, rx, 0, north)
        send(cc, rx, 2, other)
        arrive(cc, ry, 2)
        send(cc, ry, 1, east)
        send(cc, ry, 2, other)

    def corner(d):
        cc = flip(z, d) * 2 + k
        arrive(cc, rd, 0)
        arrive(cc, rd, 1)
        send(cc, rd, 2, other)

    def weigh(cc):
        start = pl.multiple_of(cc * chunk, chunk)
        logits = lax.dot_general(
            cent[...], v[pl.ds(start, chunk), :], (((1,), (1,)), ((), ())),
            preferred_element_type=jnp.float32)
        terms = jnp.exp(SHARP * logits)
        w[:, pl.ds(start, chunk)] = terms
        sums = terms[:, :LANES]
        for t in range(1, chunk // LANES):
            sums = sums + terms[:, t * LANES:(t + 1) * LANES]
        massb[...] += sums

    massb[...] = jnp.zeros_like(massb)
    own = pltpu.make_async_copy(vec, piece(c, r, 2), lsem.at[1])
    own.start()
    if depth > 1:
        send(c, r, 2, z_dev(1), vec)
    column(0)
    for e in range(2, depth):
        send(c, r, 2, z_dev(e), vec)
    own.wait()
    cent_in.wait()
    for d in range(depth):
        relay(d)
        if d + 1 < depth:
            column(d + 1)
        corner(d)
        weigh(flip(z, d) * 2 + k)
        if d:
            cc = flip(z, d - 1) * 2 + 1 - k
            for rr in range(R):
                arrive(cc, rr, 2)
            weigh(cc)
    cc = flip(z, depth - 1) * 2 + 1 - k
    for rr in range(R):
        arrive(cc, rr, 2)
    weigh(cc)

    for step in range(ROUNDS):
        if step:
            scales = [jnp.broadcast_to(row_scale[:, t * LANES:(t + 1) * LANES], (8, LANES)) for t in range(tiles)]

            def col_block(i, carry):
                at = pl.ds(pl.multiple_of(i * 8, 8), 8)
                sums = [w[at, t * LANES:(t + 1) * LANES] * scales[t] for t in range(tiles)]
                while len(sums) > 1:
                    sums = [a + b for a, b in zip(sums[::2], sums[1::2])] + ([sums[-1]] if len(sums) % 2 else [])
                massb[at, :] = sums[0]
                return carry

            lax.fori_loop(0, mine // 8, col_block, 0, unroll=8)
        mass = jnp.sum(massb[...], axis=1, keepdims=True)
        colb[...] = jnp.broadcast_to(target / mass, colb.shape)

        def row_block(i, totals):
            at = pl.ds(pl.multiple_of(i * 8, 8), 8)
            col = colb[at, :]
            return tuple(total + w[at, t * LANES:(t + 1) * LANES] * col for t, total in enumerate(totals))

        totals = lax.fori_loop(
            0, mine // 8, row_block, tuple(jnp.zeros((8, LANES), jnp.float32) for _ in range(tiles)), unroll=8)
        for t in range(tiles):
            part_a[step, :, t * LANES:(t + 1) * LANES] = jnp.sum(totals[t], axis=0, keepdims=True)

        copies = []
        for j, (q, s) in enumerate(plane):
            copy = pltpu.make_async_remote_copy(
                src_ref=part_a.at[step], dst_ref=box_a.at[step, j], send_sem=asend.at[step, j],
                recv_sem=arecv.at[step, j], device_id=plane_dev(q, s), device_id_type=MESH)
            copy.start()
            copies.append(copy)
        total = part_a[step]
        for j, copy in enumerate(copies):
            copy.wait_recv()
            total = total + box_a[step, j]
        sent.extend(copies)
        part_b[step] = total
        copies = []
        for e in range(1, depth):
            copy = pltpu.make_async_remote_copy(
                src_ref=part_b.at[step], dst_ref=box_b.at[step, e], send_sem=bsend.at[step, e],
                recv_sem=brecv.at[step, e], device_id=z_dev(e), device_id_type=MESH)
            copy.start()
            copies.append(copy)
        for e, copy in enumerate(copies):
            copy.wait_recv()
            total = total + box_b[step, e + 1]
        sent.extend(copies)
        row_scale = 1.0 / total

    scales = [jnp.broadcast_to(row_scale[:, t * LANES:(t + 1) * LANES], (16, LANES)) for t in range(tiles)]

    def block(i, carry):
        at = pl.ds(pl.multiple_of(i * 16, 16), 16)
        col = colb[at, :]
        mass = jnp.zeros((16, LANES), jnp.float32)
        for t in range(tiles):
            term = w[at, t * LANES:(t + 1) * LANES] * scales[t] * col
            mass = mass + term
            plan[at, t * LANES:(t + 1) * LANES] = term.astype(jnp.bfloat16)
        massb[at, :] = mass
        return carry

    lax.fori_loop(0, mine // 16, block, 0, unroll=4)
    massb[...] = jnp.broadcast_to(jnp.sum(massb[...], axis=1, keepdims=True), massb.shape)

    width = out.shape[1]
    results = []
    for q in (3, 1, 2, 0):
        peer = flip(r, q)
        cols = pl.ds(pl.multiple_of(peer * width, width), width)
        sums = jnp.dot(plan[...], v[:, cols], preferred_element_type=jnp.float32)
        mass = jnp.concatenate([massb[...]] * (width // LANES), axis=1)
        outbuf[q] = (0.5 * cent[:, cols].astype(jnp.float32) + 0.5 * sums / mass).astype(jnp.bfloat16)
        dst = out.at[pl.ds(pl.multiple_of(r * mine, mine), mine), :]
        if q:
            copy = pltpu.make_async_remote_copy(
                src_ref=outbuf.at[q], dst_ref=dst, send_sem=osend.at[q], recv_sem=orecv.at[q],
                device_id=(peer, c), device_id_type=MESH)
        else:
            copy = pltpu.make_async_copy(outbuf.at[q], dst, lsem.at[2])
        copy.start()
        results.append((q, copy))

    massrow[...] = jnp.transpose(massb[...], (1, 0))[:1, :]
    mdst = mass_out.at[r]
    mcopies = []
    for q in range(1, R):
        copy = pltpu.make_async_remote_copy(
            src_ref=massrow, dst_ref=mdst, send_sem=msend.at[q], recv_sem=mrecv.at[q],
            device_id=(flip(r, q), c), device_id_type=MESH)
        copy.start()
        mcopies.append(copy)
    local = pltpu.make_async_copy(massrow, mdst, lsem.at[3])
    local.start()

    for copy in sent:
        copy.wait_send()
    local.wait()
    for copy in mcopies:
        copy.wait()
    for q, copy in results:
        copy.wait()


def body(vectors, centroids, shards):
    rows, embed = vectors.shape
    batch = rows * R * shards
    held = centroids.shape[0]
    mine = held // R
    width = embed // R
    target = batch / (held * shards)
    depth = shards // 2
    f32, bf16 = jnp.float32, jnp.bfloat16
    dma = pltpu.SemaphoreType.DMA
    limit = 56 << 20
    updated, masses = pl.pallas_call(
        functools.partial(kernel, shards, target),
        out_shape=(jax.ShapeDtypeStruct((held, width), bf16), jax.ShapeDtypeStruct((R, 1, mine), f32)),
        in_specs=[pl.BlockSpec(memory_space=pltpu.VMEM), pl.BlockSpec(memory_space=pl.ANY)],
        out_specs=(pl.BlockSpec(memory_space=pl.ANY), pl.BlockSpec(memory_space=pl.ANY)),
        scratch_shapes=[
            pltpu.VMEM((batch, embed), bf16),
            pltpu.VMEM((mine, batch), f32),
            pltpu.VMEM((mine, batch), bf16),
            pltpu.VMEM((mine, embed), bf16),
            pltpu.VMEM((mine, LANES), f32),
            pltpu.VMEM((mine, LANES), f32),
            pltpu.VMEM((1, mine), f32),
            pltpu.VMEM((R, mine, width), bf16),
            pltpu.VMEM((ROUNDS, 1, batch), f32),
            pltpu.VMEM((ROUNDS, 1, batch), f32),
            pltpu.VMEM((ROUNDS, 2 * R - 1, 1, batch), f32),
            pltpu.VMEM((ROUNDS, depth, 1, batch), f32),
            dma((depth * 9,)), dma((shards * R * 2,)),
            dma((ROUNDS, 2 * R)), dma((ROUNDS, 2 * R)),
            dma((ROUNDS, depth)), dma((ROUNDS, depth)),
            dma((R,)), dma((R,)), dma((R,)), dma((R,)), dma((4,)),
        ],
        compiler_params=pltpu.CompilerParams(
            collective_id=0, has_side_effects=True, vmem_limit_bytes=limit),
        cost_estimate=pl.CostEstimate(
            flops=4 * mine * batch * embed, bytes_accessed=2 * mine * embed * 4, transcendentals=mine * batch),
    )(vectors, centroids)
    return updated, masses.reshape(held)


def solution(mesh):
    from jax.sharding import PartitionSpec as P
    return jax.shard_map(
        functools.partial(body, shards=mesh.shape["cents"]),
        mesh=mesh,
        in_specs=(P(("rows", "cents"), None), P("cents", None)),
        out_specs=(P("cents", "rows"), P("cents")),
        check_vma=False,
    )
```

```python
import functools

import jax
import jax.numpy as jnp
from jax import lax
from jax.experimental import pallas as pl
from jax.experimental.pallas import tpu as pltpu

ROUNDS = 3
SHARP = 0.75
R = 4
LANES = 128
MESH = pl.DeviceIdType.MESH


def flip(a, d):
    out, bit = a, 1
    while bit <= d:
        if d & bit:
            out = out + bit - 2 * bit * lax.rem(lax.div(out, bit), 2)
        bit *= 2
    return out


def kernel(shards, target, vec, cent_hbm, out, mass_out, v, w, plan, cent, colb, massb, massrow, outbuf,
           part_a, part_b, box_a, box_b,
           gsend, psend, grecv, asend, arecv, bsend, brecv, osend, orecv, msend, mrecv, lsem):
    r, c = lax.axis_index("rows"), lax.axis_index("cents")
    z, k = lax.div(c, 2), lax.rem(c, 2)
    depth = shards // 2
    rows = vec.shape[0]
    half = rows // 2
    mine = cent.shape[0]
    batch = v.shape[0]
    chunk = R * rows
    tiles = batch // LANES

    plane = [(q, s) for q in range(R) for s in range(2) if (q, s) != (0, 0)]

    def plane_dev(q, s):
        return (flip(r, q), flip(c, s))

    def z_dev(e):
        return (r, flip(z, e) * 2 + k)

    barrier = pltpu.get_barrier_semaphore()
    for q, s in plane:
        pl.semaphore_signal(barrier, inc=1, device_id=plane_dev(q, s), device_id_type=MESH)
    for e in range(1, depth):
        pl.semaphore_signal(barrier, inc=1, device_id=z_dev(e), device_id_type=MESH)
    cent_in = pltpu.make_async_copy(
        cent_hbm.at[pl.ds(pl.multiple_of(r * mine, mine), mine), :], cent, lsem.at[0])
    cent_in.start()
    pl.semaphore_wait(barrier, len(plane) + depth - 1)

    sent = []

    def piece(cc, rr, part):
        base = (cc * R + rr) * rows
        if part == 2:
            return v.at[pl.ds(pl.multiple_of(base, rows), rows), :]
        return v.at[pl.ds(pl.multiple_of(base + part * half, half), half), :]

    def gsem(cc, rr, part):
        return grecv.at[(cc * R + rr) * 2 + (0 if part == 2 else part)]

    def send(cc, rr, part, dev, src=None):
        copy = pltpu.make_async_remote_copy(
            src_ref=piece(cc, rr, part) if src is None else src,
            dst_ref=piece(cc, rr, part),
            send_sem=gsend.at[len(sent)],
            recv_sem=gsem(cc, rr, part),
            device_id=dev, device_id_type=MESH)
        copy.start()
        sent.append(copy)

    def arrive(cc, rr, part):
        ref = piece(cc, rr, part)
        pltpu.make_async_remote_copy(
            src_ref=ref, dst_ref=ref, send_sem=gsend.at[0], recv_sem=gsem(cc, rr, part),
            device_id=plane_dev(0, 1), device_id_type=MESH).wait_recv()

    east, north, other = plane_dev(1, 0), plane_dev(2, 0), plane_dev(0, 1)
    rx, ry, rd = flip(r, 1), flip(r, 2), flip(r, 3)

    line = depth == 4
    inner = lax.rem(lax.div(z + 1, 2), 2)

    def source(d):
        if line and d >= 2:
            return inner * flip(z, 5 - d) + (1 - inner) * flip(z, d)
        return flip(z, d)

    passed = []

    def pass_on(cc, e, src=None):
        n = len(passed)
        copy = pltpu.make_async_remote_copy(
            src_ref=piece(cc, r, 2) if src is None else src,
            dst_ref=piece(cc, r, 2),
            send_sem=psend.at[n], recv_sem=gsem(cc, r, 2),
            device_id=z_dev(e), device_id_type=MESH)
        passed.append(copy)

        @pl.when(inner == 1)
        def _():
            copy.start()

    def column(d):
        cc = source(d) * 2 + k
        if d:
            arrive(cc, r, 2)
            if line:
                pass_on(cc, 3 if d == 1 else 1)
        src = None if d else vec
        send(cc, r, 2, east, src)
        send(cc, r, 2, north, src)
        send(cc, r, 2, other, src)

    def relay(d):
        cc = source(d) * 2 + k
        arrive(cc, rx, 2)
        send(cc, rx, 0, north)
        send(cc, rx, 2, other)
        arrive(cc, ry, 2)
        send(cc, ry, 1, east)
        send(cc, ry, 2, other)

    def corner(d):
        cc = source(d) * 2 + k
        arrive(cc, rd, 0)
        arrive(cc, rd, 1)
        send(cc, rd, 2, other)

    def weigh(cc):
        start = pl.multiple_of(cc * chunk, chunk)
        logits = lax.dot_general(
            cent[...], v[pl.ds(start, chunk), :], (((1,), (1,)), ((), ())),
            preferred_element_type=jnp.float32)
        terms = jnp.exp(SHARP * logits)
        w[:, pl.ds(start, chunk)] = terms
        sums = terms[:, :LANES]
        for t in range(1, chunk // LANES):
            sums = sums + terms[:, t * LANES:(t + 1) * LANES]
        massb[...] += sums

    massb[...] = jnp.zeros_like(massb)
    own = pltpu.make_async_copy(vec, piece(c, r, 2), lsem.at[1])
    own.start()
    if depth > 1:
        send(c, r, 2, z_dev(1), vec)
    if line:
        pass_on(c, 3, vec)
    column(0)
    if not line:
        for e in range(2, depth):
            send(c, r, 2, z_dev(e), vec)
    own.wait()
    cent_in.wait()

    def partner(d):
        cc = source(d) * 2 + 1 - k
        for rr in range(R):
            arrive(cc, rr, 2)
        weigh(cc)

    for d in range(depth):
        relay(d)
        if d + 1 < depth:
            column(d + 1)
        if d:
            partner(d - 1)
        corner(d)
        weigh(source(d) * 2 + k)
    partner(depth - 1)

    for step in range(ROUNDS):
        if step:
            scales = [jnp.broadcast_to(row_scale[:, t * LANES:(t + 1) * LANES], (8, LANES)) for t in range(tiles)]

            def col_block(i, carry):
                at = pl.ds(pl.multiple_of(i * 8, 8), 8)
                sums = [w[at, t * LANES:(t + 1) * LANES] * scales[t] for t in range(tiles)]
                while len(sums) > 1:
                    sums = [a + b for a, b in zip(sums[::2], sums[1::2])] + ([sums[-1]] if len(sums) % 2 else [])
                massb[at, :] = sums[0]
                return carry

            lax.fori_loop(0, mine // 8, col_block, 0, unroll=8)
        mass = jnp.sum(massb[...], axis=1, keepdims=True)
        colb[...] = jnp.broadcast_to(target / mass, colb.shape)

        def row_block(i, totals):
            at = pl.ds(pl.multiple_of(i * 8, 8), 8)
            col = colb[at, :]
            return tuple(total + w[at, t * LANES:(t + 1) * LANES] * col for t, total in enumerate(totals))

        totals = lax.fori_loop(
            0, mine // 8, row_block, tuple(jnp.zeros((8, LANES), jnp.float32) for _ in range(tiles)), unroll=8)
        for t in range(tiles):
            part_a[step, :, t * LANES:(t + 1) * LANES] = jnp.sum(totals[t], axis=0, keepdims=True)

        copies = []
        for j, (q, s) in enumerate(plane):
            copy = pltpu.make_async_remote_copy(
                src_ref=part_a.at[step], dst_ref=box_a.at[step, j], send_sem=asend.at[step, j],
                recv_sem=arecv.at[step, j], device_id=plane_dev(q, s), device_id_type=MESH)
            copy.start()
            copies.append(copy)
        total = part_a[step]
        for j, copy in enumerate(copies):
            copy.wait_recv()
            total = total + box_a[step, j]
        sent.extend(copies)
        part_b[step] = total
        copies = []
        for e in range(1, depth):
            copy = pltpu.make_async_remote_copy(
                src_ref=part_b.at[step], dst_ref=box_b.at[step, e], send_sem=bsend.at[step, e],
                recv_sem=brecv.at[step, e], device_id=z_dev(e), device_id_type=MESH)
            copy.start()
            copies.append(copy)
        for e, copy in enumerate(copies):
            copy.wait_recv()
            total = total + box_b[step, e + 1]
        sent.extend(copies)
        row_scale = 1.0 / total

    scales = [jnp.broadcast_to(row_scale[:, t * LANES:(t + 1) * LANES], (16, LANES)) for t in range(tiles)]

    def block(i, carry):
        at = pl.ds(pl.multiple_of(i * 16, 16), 16)
        col = colb[at, :]
        mass = jnp.zeros((16, LANES), jnp.float32)
        for t in range(tiles):
            term = w[at, t * LANES:(t + 1) * LANES] * scales[t] * col
            mass = mass + term
            plan[at, t * LANES:(t + 1) * LANES] = term.astype(jnp.bfloat16)
        massb[at, :] = mass
        return carry

    lax.fori_loop(0, mine // 16, block, 0, unroll=4)
    massb[...] = jnp.broadcast_to(jnp.sum(massb[...], axis=1, keepdims=True), massb.shape)

    width = out.shape[1]
    results = []
    for q in (3, 1, 2, 0):
        peer = flip(r, q)
        cols = pl.ds(pl.multiple_of(peer * width, width), width)
        sums = jnp.dot(plan[...], v[:, cols], preferred_element_type=jnp.float32)
        mass = jnp.concatenate([massb[...]] * (width // LANES), axis=1)
        outbuf[q] = (0.5 * cent[:, cols].astype(jnp.float32) + 0.5 * sums / mass).astype(jnp.bfloat16)
        dst = out.at[pl.ds(pl.multiple_of(r * mine, mine), mine), :]
        if q:
            copy = pltpu.make_async_remote_copy(
                src_ref=outbuf.at[q], dst_ref=dst, send_sem=osend.at[q], recv_sem=orecv.at[q],
                device_id=(peer, c), device_id_type=MESH)
        else:
            copy = pltpu.make_async_copy(outbuf.at[q], dst, lsem.at[2])
        copy.start()
        results.append((q, copy))

    massrow[...] = jnp.transpose(massb[...], (1, 0))[:1, :]
    mdst = mass_out.at[r]
    mcopies = []
    for q in range(1, R):
        copy = pltpu.make_async_remote_copy(
            src_ref=massrow, dst_ref=mdst, send_sem=msend.at[q], recv_sem=mrecv.at[q],
            device_id=(flip(r, q), c), device_id_type=MESH)
        copy.start()
        mcopies.append(copy)
    local = pltpu.make_async_copy(massrow, mdst, lsem.at[3])
    local.start()

    for copy in sent:
        copy.wait_send()
    if passed:
        @pl.when(inner == 1)
        def _():
            for copy in passed:
                copy.wait_send()
    local.wait()
    for copy in mcopies:
        copy.wait()
    for q, copy in results:
        copy.wait()


def body(vectors, centroids, shards):
    rows, embed = vectors.shape
    batch = rows * R * shards
    held = centroids.shape[0]
    mine = held // R
    width = embed // R
    target = batch / (held * shards)
    depth = shards // 2
    f32, bf16 = jnp.float32, jnp.bfloat16
    dma = pltpu.SemaphoreType.DMA
    limit = 51 << 20
    updated, masses = pl.pallas_call(
        functools.partial(kernel, shards, target),
        out_shape=(jax.ShapeDtypeStruct((held, width), bf16), jax.ShapeDtypeStruct((R, 1, mine), f32)),
        in_specs=[pl.BlockSpec(memory_space=pltpu.VMEM), pl.BlockSpec(memory_space=pl.ANY)],
        out_specs=(pl.BlockSpec(memory_space=pl.ANY), pl.BlockSpec(memory_space=pl.ANY)),
        scratch_shapes=[
            pltpu.VMEM((batch, embed), bf16),
            pltpu.VMEM((mine, batch), f32),
            pltpu.VMEM((mine, batch), bf16),
            pltpu.VMEM((mine, embed), bf16),
            pltpu.VMEM((mine, LANES), f32),
            pltpu.VMEM((mine, LANES), f32),
            pltpu.VMEM((1, mine), f32),
            pltpu.VMEM((R, mine, width), bf16),
            pltpu.VMEM((ROUNDS, 1, batch), f32),
            pltpu.VMEM((ROUNDS, 1, batch), f32),
            pltpu.VMEM((ROUNDS, 2 * R - 1, 1, batch), f32),
            pltpu.VMEM((ROUNDS, depth, 1, batch), f32),
            dma((depth * 9,)), dma((4,)), dma((shards * R * 2,)),
            dma((ROUNDS, 2 * R)), dma((ROUNDS, 2 * R)),
            dma((ROUNDS, depth)), dma((ROUNDS, depth)),
            dma((R,)), dma((R,)), dma((R,)), dma((R,)), dma((4,)),
        ],
        compiler_params=pltpu.CompilerParams(
            collective_id=0, has_side_effects=True, vmem_limit_bytes=limit),
        cost_estimate=pl.CostEstimate(
            flops=4 * mine * batch * embed, bytes_accessed=2 * mine * embed * 4, transcendentals=mine * batch),
    )(vectors, centroids)
    return updated, masses.reshape(held)


def solution(mesh):
    from jax.sharding import PartitionSpec as P
    return jax.shard_map(
        functools.partial(body, shards=mesh.shape["cents"]),
        mesh=mesh,
        in_specs=(P(("rows", "cents"), None), P("cents", None)),
        out_specs=(P("cents", "rows"), P("cents")),
        check_vma=False,
    )
```

```python
import functools

import jax
import jax.numpy as jnp
from jax import lax
from jax.experimental import pallas as pl
from jax.experimental.pallas import tpu as pltpu

ROUNDS = 3
SHARP = 0.75
R = 4
LANES = 128
MESH = pl.DeviceIdType.MESH


def flip(a, d):
    out, bit = a, 1
    while bit <= d:
        if d & bit:
            out = out + bit - 2 * bit * lax.rem(lax.div(out, bit), 2)
        bit *= 2
    return out


def kernel(shards, target, vec, cent_hbm, out, mass_out, v, w, plan, cent, colb, massb, massrow, outbuf,
           part_a, part_b, box_a, box_b,
           gsend, psend, grecv, asend, arecv, bsend, brecv, osend, orecv, msend, mrecv, lsem):
    r, c = lax.axis_index("rows"), lax.axis_index("cents")
    z, k = lax.div(c, 2), lax.rem(c, 2)
    depth = shards // 2
    rows = vec.shape[0]
    half = rows // 2
    mine = cent.shape[0]
    batch = v.shape[0]
    chunk = R * rows
    tiles = batch // LANES

    plane = [(q, s) for q in range(R) for s in range(2) if (q, s) != (0, 0)]

    def plane_dev(q, s):
        return (flip(r, q), flip(c, s))

    def z_dev(e):
        return (r, flip(z, e) * 2 + k)

    barrier = pltpu.get_barrier_semaphore()
    for q, s in plane:
        pl.semaphore_signal(barrier, inc=1, device_id=plane_dev(q, s), device_id_type=MESH)
    for e in range(1, depth):
        pl.semaphore_signal(barrier, inc=1, device_id=z_dev(e), device_id_type=MESH)
    cent_in = pltpu.make_async_copy(
        cent_hbm.at[pl.ds(pl.multiple_of(r * mine, mine), mine), :], cent, lsem.at[0])
    cent_in.start()
    pl.semaphore_wait(barrier, len(plane) + depth - 1)

    sent = []

    def piece(cc, rr, part):
        base = (cc * R + rr) * rows
        if part == 2:
            return v.at[pl.ds(pl.multiple_of(base, rows), rows), :]
        return v.at[pl.ds(pl.multiple_of(base + part * half, half), half), :]

    def gsem(cc, rr, part):
        return grecv.at[(cc * R + rr) * 2 + (0 if part == 2 else part)]

    def send(cc, rr, part, dev, src=None):
        copy = pltpu.make_async_remote_copy(
            src_ref=piece(cc, rr, part) if src is None else src,
            dst_ref=piece(cc, rr, part),
            send_sem=gsend.at[len(sent)],
            recv_sem=gsem(cc, rr, part),
            device_id=dev, device_id_type=MESH)
        copy.start()
        sent.append(copy)

    def arrive(cc, rr, part):
        ref = piece(cc, rr, part)
        pltpu.make_async_remote_copy(
            src_ref=ref, dst_ref=ref, send_sem=gsend.at[0], recv_sem=gsem(cc, rr, part),
            device_id=plane_dev(0, 1), device_id_type=MESH).wait_recv()

    east, north, other = plane_dev(1, 0), plane_dev(2, 0), plane_dev(0, 1)
    rx, ry, rd = flip(r, 1), flip(r, 2), flip(r, 3)

    line = depth == 4
    inner = lax.rem(lax.div(z + 1, 2), 2)

    def source(d):
        if line and d >= 2:
            return inner * flip(z, 5 - d) + (1 - inner) * flip(z, d)
        return flip(z, d)

    passed = []

    def pass_on(cc, e, src=None):
        n = len(passed)
        copy = pltpu.make_async_remote_copy(
            src_ref=piece(cc, r, 2) if src is None else src,
            dst_ref=piece(cc, r, 2),
            send_sem=psend.at[n], recv_sem=gsem(cc, r, 2),
            device_id=z_dev(e), device_id_type=MESH)
        passed.append(copy)

        @pl.when(inner == 1)
        def _():
            copy.start()

    def column(d):
        cc = source(d) * 2 + k
        if d:
            arrive(cc, r, 2)
            if line:
                pass_on(cc, 3 if d == 1 else 1)
        src = None if d else vec
        send(cc, r, 2, east, src)
        send(cc, r, 2, north, src)
        send(cc, r, 2, other, src)

    def relay(d):
        cc = source(d) * 2 + k
        arrive(cc, rx, 2)
        send(cc, rx, 0, north)
        send(cc, rx, 2, other)
        arrive(cc, ry, 2)
        send(cc, ry, 1, east)
        send(cc, ry, 2, other)

    def corner(d):
        cc = source(d) * 2 + k
        arrive(cc, rd, 0)
        arrive(cc, rd, 1)
        send(cc, rd, 2, other)

    def weigh(cc):
        start = pl.multiple_of(cc * chunk, chunk)
        logits = lax.dot_general(
            cent[...], v[pl.ds(start, chunk), :], (((1,), (1,)), ((), ())),
            preferred_element_type=jnp.float32)
        terms = jnp.exp(SHARP * logits)
        w[:, pl.ds(start, chunk)] = terms
        sums = terms[:, :LANES]
        for t in range(1, chunk // LANES):
            sums = sums + terms[:, t * LANES:(t + 1) * LANES]
        massb[...] += sums

    massb[...] = jnp.zeros_like(massb)
    own = pltpu.make_async_copy(vec, piece(c, r, 2), lsem.at[1])
    own.start()
    if depth > 1:
        send(c, r, 2, z_dev(1), vec)
    if line:
        pass_on(c, 3, vec)
    column(0)
    if not line:
        for e in range(2, depth):
            send(c, r, 2, z_dev(e), vec)
    own.wait()
    cent_in.wait()

    def partner(d):
        cc = source(d) * 2 + 1 - k
        for rr in range(R):
            arrive(cc, rr, 2)
        weigh(cc)

    if depth > 1:
        column(1)
    for d in range(depth):
        relay(d)
        if d + 2 < depth:
            column(d + 2)
        if d:
            partner(d - 1)
        corner(d)
        weigh(source(d) * 2 + k)
    partner(depth - 1)

    for step in range(ROUNDS):
        if step:
            scales = [jnp.broadcast_to(row_scale[t:t + 1, :], (8, LANES)) for t in range(tiles)]

            def col_block(i, carry):
                at = pl.ds(pl.multiple_of(i * 8, 8), 8)
                sums = [w[at, t * LANES:(t + 1) * LANES] * scales[t] for t in range(tiles)]
                while len(sums) > 1:
                    sums = [a + b for a, b in zip(sums[::2], sums[1::2])] + ([sums[-1]] if len(sums) % 2 else [])
                massb[at, :] = sums[0]
                return carry

            lax.fori_loop(0, mine // 8, col_block, 0, unroll=8)
        mass = jnp.sum(massb[...], axis=1, keepdims=True)
        colb[...] = jnp.broadcast_to(target / mass, colb.shape)

        def row_block(i, totals):
            at = pl.ds(pl.multiple_of(i * 8, 8), 8)
            col = colb[at, :]
            return tuple(total + w[at, t * LANES:(t + 1) * LANES] * col for t, total in enumerate(totals))

        totals = lax.fori_loop(
            0, mine // 8, row_block, tuple(jnp.zeros((8, LANES), jnp.float32) for _ in range(tiles)), unroll=8)
        total = jnp.concatenate([jnp.sum(part, axis=0, keepdims=True) for part in totals], axis=0)

        part_a[step] = total.astype(jnp.bfloat16)
        copies = []
        for j, (q, s) in enumerate(plane):
            copy = pltpu.make_async_remote_copy(
                src_ref=part_a.at[step], dst_ref=box_a.at[step, j], send_sem=asend.at[step, j],
                recv_sem=arecv.at[step, j], device_id=plane_dev(q, s), device_id_type=MESH)
            copy.start()
            copies.append(copy)
        for j, copy in enumerate(copies):
            copy.wait_recv()
            total = total + box_a[step, j].astype(jnp.float32)
        sent.extend(copies)
        part_b[step] = total.astype(jnp.bfloat16)
        copies = []
        for e in range(1, depth):
            copy = pltpu.make_async_remote_copy(
                src_ref=part_b.at[step], dst_ref=box_b.at[step, e], send_sem=bsend.at[step, e],
                recv_sem=brecv.at[step, e], device_id=z_dev(e), device_id_type=MESH)
            copy.start()
            copies.append(copy)
        for e, copy in enumerate(copies):
            copy.wait_recv()
            total = total + box_b[step, e + 1].astype(jnp.float32)
        sent.extend(copies)
        row_scale = 1.0 / total

    scales = [jnp.broadcast_to(row_scale[t:t + 1, :], (16, LANES)) for t in range(tiles)]

    def block(i, carry):
        at = pl.ds(pl.multiple_of(i * 16, 16), 16)
        col = colb[at, :]
        mass = jnp.zeros((16, LANES), jnp.float32)
        for t in range(tiles):
            term = w[at, t * LANES:(t + 1) * LANES] * scales[t] * col
            mass = mass + term
            plan[at, t * LANES:(t + 1) * LANES] = term.astype(jnp.bfloat16)
        massb[at, :] = mass
        return carry

    lax.fori_loop(0, mine // 16, block, 0, unroll=4)
    massb[...] = jnp.broadcast_to(jnp.sum(massb[...], axis=1, keepdims=True), massb.shape)

    width = out.shape[1]
    results = []
    for q in (3, 1, 2, 0):
        peer = flip(r, q)
        cols = pl.ds(pl.multiple_of(peer * width, width), width)
        sums = jnp.dot(plan[...], v[:, cols], preferred_element_type=jnp.float32)
        mass = jnp.concatenate([massb[...]] * (width // LANES), axis=1)
        outbuf[q] = (0.5 * cent[:, cols].astype(jnp.float32) + 0.5 * sums / mass).astype(jnp.bfloat16)
        dst = out.at[pl.ds(pl.multiple_of(r * mine, mine), mine), :]
        if q:
            copy = pltpu.make_async_remote_copy(
                src_ref=outbuf.at[q], dst_ref=dst, send_sem=osend.at[q], recv_sem=orecv.at[q],
                device_id=(peer, c), device_id_type=MESH)
        else:
            copy = pltpu.make_async_copy(outbuf.at[q], dst, lsem.at[2])
        copy.start()
        results.append((q, copy))

    massrow[...] = jnp.transpose(massb[...], (1, 0))[:1, :]
    mdst = mass_out.at[r]
    mcopies = []
    for q in range(1, R):
        copy = pltpu.make_async_remote_copy(
            src_ref=massrow, dst_ref=mdst, send_sem=msend.at[q], recv_sem=mrecv.at[q],
            device_id=(flip(r, q), c), device_id_type=MESH)
        copy.start()
        mcopies.append(copy)
    local = pltpu.make_async_copy(massrow, mdst, lsem.at[3])
    local.start()

    for copy in sent:
        copy.wait_send()
    if passed:
        @pl.when(inner == 1)
        def _():
            for copy in passed:
                copy.wait_send()
    local.wait()
    for copy in mcopies:
        copy.wait()
    for q, copy in results:
        copy.wait()


def body(vectors, centroids, shards):
    rows, embed = vectors.shape
    batch = rows * R * shards
    held = centroids.shape[0]
    mine = held // R
    width = embed // R
    target = batch / (held * shards)
    depth = shards // 2
    tiles = batch // LANES
    f32, bf16 = jnp.float32, jnp.bfloat16
    dma = pltpu.SemaphoreType.DMA
    limit = 51 << 20
    updated, masses = pl.pallas_call(
        functools.partial(kernel, shards, target),
        out_shape=(jax.ShapeDtypeStruct((held, width), bf16), jax.ShapeDtypeStruct((R, 1, mine), f32)),
        in_specs=[pl.BlockSpec(memory_space=pltpu.VMEM), pl.BlockSpec(memory_space=pl.ANY)],
        out_specs=(pl.BlockSpec(memory_space=pl.ANY), pl.BlockSpec(memory_space=pl.ANY)),
        scratch_shapes=[
            pltpu.VMEM((batch, embed), bf16),
            pltpu.VMEM((mine, batch), f32),
            pltpu.VMEM((mine, batch), bf16),
            pltpu.VMEM((mine, embed), bf16),
            pltpu.VMEM((mine, LANES), f32),
            pltpu.VMEM((mine, LANES), f32),
            pltpu.VMEM((1, mine), f32),
            pltpu.VMEM((R, mine, width), bf16),
            pltpu.VMEM((ROUNDS, tiles, LANES), bf16),
            pltpu.VMEM((ROUNDS, tiles, LANES), bf16),
            pltpu.VMEM((ROUNDS, 2 * R - 1, tiles, LANES), bf16),
            pltpu.VMEM((ROUNDS, depth, tiles, LANES), bf16),
            dma((depth * 9,)), dma((4,)), dma((shards * R * 2,)),
            dma((ROUNDS, 2 * R)), dma((ROUNDS, 2 * R)),
            dma((ROUNDS, depth)), dma((ROUNDS, depth)),
            dma((R,)), dma((R,)), dma((R,)), dma((R,)), dma((4,)),
        ],
        compiler_params=pltpu.CompilerParams(
            collective_id=0, has_side_effects=True, vmem_limit_bytes=limit),
        cost_estimate=pl.CostEstimate(
            flops=4 * mine * batch * embed, bytes_accessed=2 * mine * embed * 4, transcendentals=mine * batch),
    )(vectors, centroids)
    return updated, masses.reshape(held)


def solution(mesh):
    from jax.sharding import PartitionSpec as P
    return jax.shard_map(
        functools.partial(body, shards=mesh.shape["cents"]),
        mesh=mesh,
        in_specs=(P(("rows", "cents"), None), P("cents", None)),
        out_specs=(P("cents", "rows"), P("cents")),
        check_vma=False,
    )
```

```python
import functools

import jax
import jax.numpy as jnp
from jax import lax
from jax.experimental import pallas as pl
from jax.experimental.pallas import tpu as pltpu

ROUNDS = 3
SHARP = 0.75
R = 4
LANES = 128
MESH = pl.DeviceIdType.MESH


def flip(a, d):
    out, bit = a, 1
    while bit <= d:
        if d & bit:
            out = out + bit - 2 * bit * lax.rem(lax.div(out, bit), 2)
        bit *= 2
    return out


def kernel(shards, target, vec, cent_hbm, out, mass_out, v, w, plan, cent, colb, massb, massrow, outbuf,
           part_a, part_b, box_a, box_b,
           gsend, psend, grecv, asend, arecv, bsend, brecv, osend, orecv, msend, mrecv, lsem):
    r, c = lax.axis_index("rows"), lax.axis_index("cents")
    z, k = lax.div(c, 2), lax.rem(c, 2)
    depth = shards // 2
    rows = vec.shape[0]
    half = rows // 2
    mine = cent.shape[0]
    batch = v.shape[0]
    chunk = R * rows
    tiles = batch // LANES

    plane = [(3, 1), (3, 0), (2, 1), (1, 1), (2, 0), (1, 0), (0, 1)]

    def plane_dev(q, s):
        return (flip(r, q), flip(c, s))

    def z_dev(e):
        return (r, flip(z, e) * 2 + k)

    barrier = pltpu.get_barrier_semaphore()
    for q, s in plane:
        pl.semaphore_signal(barrier, inc=1, device_id=plane_dev(q, s), device_id_type=MESH)
    for e in range(1, depth):
        pl.semaphore_signal(barrier, inc=1, device_id=z_dev(e), device_id_type=MESH)
    cent_in = pltpu.make_async_copy(
        cent_hbm.at[pl.ds(pl.multiple_of(r * mine, mine), mine), :], cent, lsem.at[0])
    cent_in.start()
    pl.semaphore_wait(barrier, len(plane) + depth - 1)

    sent = []

    def piece(cc, rr, part):
        base = (cc * R + rr) * rows
        if part == 2:
            return v.at[pl.ds(pl.multiple_of(base, rows), rows), :]
        return v.at[pl.ds(pl.multiple_of(base + part * half, half), half), :]

    def gsem(cc, rr, part):
        return grecv.at[(cc * R + rr) * 2 + (0 if part == 2 else part)]

    def send(cc, rr, part, dev, src=None):
        copy = pltpu.make_async_remote_copy(
            src_ref=piece(cc, rr, part) if src is None else src,
            dst_ref=piece(cc, rr, part),
            send_sem=gsend.at[len(sent)],
            recv_sem=gsem(cc, rr, part),
            device_id=dev, device_id_type=MESH)
        copy.start()
        sent.append(copy)

    def arrive(cc, rr, part):
        ref = piece(cc, rr, part)
        pltpu.make_async_remote_copy(
            src_ref=ref, dst_ref=ref, send_sem=gsend.at[0], recv_sem=gsem(cc, rr, part),
            device_id=plane_dev(0, 1), device_id_type=MESH).wait_recv()

    east, north, other = plane_dev(1, 0), plane_dev(2, 0), plane_dev(0, 1)
    rx, ry, rd = flip(r, 1), flip(r, 2), flip(r, 3)

    line = depth == 4
    inner = lax.rem(lax.div(z + 1, 2), 2)

    def source(d):
        if line and d >= 2:
            return inner * flip(z, 5 - d) + (1 - inner) * flip(z, d)
        return flip(z, d)

    passed = []

    def pass_on(cc, e, src=None):
        n = len(passed)
        copy = pltpu.make_async_remote_copy(
            src_ref=piece(cc, r, 2) if src is None else src,
            dst_ref=piece(cc, r, 2),
            send_sem=psend.at[n], recv_sem=gsem(cc, r, 2),
            device_id=z_dev(e), device_id_type=MESH)
        passed.append(copy)

        @pl.when(inner == 1)
        def _():
            copy.start()

    def column(d):
        cc = source(d) * 2 + k
        if d:
            arrive(cc, r, 2)
            if line:
                pass_on(cc, 3 if d == 1 else 1)
        src = None if d else vec
        send(cc, r, 2, east, src)
        send(cc, r, 2, north, src)
        send(cc, r, 2, other, src)

    def relay(d):
        cc = source(d) * 2 + k
        arrive(cc, rx, 2)
        send(cc, rx, 0, north)
        send(cc, rx, 2, other)
        arrive(cc, ry, 2)
        send(cc, ry, 1, east)
        send(cc, ry, 2, other)

    def corner(d):
        cc = source(d) * 2 + k
        arrive(cc, rd, 0)
        arrive(cc, rd, 1)
        send(cc, rd, 2, other)

    def weigh(cc):
        start = pl.multiple_of(cc * chunk, chunk)
        logits = lax.dot_general(
            cent[...], v[pl.ds(start, chunk), :], (((1,), (1,)), ((), ())),
            preferred_element_type=jnp.float32)
        terms = jnp.exp(SHARP * logits)
        w[:, pl.ds(start, chunk)] = terms
        sums = terms[:, :LANES]
        for t in range(1, chunk // LANES):
            sums = sums + terms[:, t * LANES:(t + 1) * LANES]
        massb[...] += sums

    massb[...] = jnp.zeros_like(massb)
    own = pltpu.make_async_copy(vec, piece(c, r, 2), lsem.at[1])
    own.start()
    if depth > 1:
        send(c, r, 2, z_dev(1), vec)
    if line:
        pass_on(c, 3, vec)
    column(0)
    if not line:
        for e in range(2, depth):
            send(c, r, 2, z_dev(e), vec)
    own.wait()
    cent_in.wait()

    def partner(d):
        cc = source(d) * 2 + 1 - k
        for rr in range(R):
            arrive(cc, rr, 2)
        weigh(cc)

    if depth > 1:
        column(1)
    relay(0)
    for d in range(depth):
        if d + 2 < depth:
            column(d + 2)
        if d + 1 < depth:
            relay(d + 1)
        if d:
            partner(d - 1)
        corner(d)
        weigh(source(d) * 2 + k)
    partner(depth - 1)

    for step in range(ROUNDS):
        if step:
            scales = [jnp.broadcast_to(row_scale[t:t + 1, :], (8, LANES)) for t in range(tiles)]

            def col_block(i, carry):
                at = pl.ds(pl.multiple_of(i * 8, 8), 8)
                sums = [w[at, t * LANES:(t + 1) * LANES] * scales[t] for t in range(tiles)]
                while len(sums) > 1:
                    sums = [a + b for a, b in zip(sums[::2], sums[1::2])] + ([sums[-1]] if len(sums) % 2 else [])
                massb[at, :] = sums[0]
                return carry

            lax.fori_loop(0, mine // 8, col_block, 0, unroll=8)
        mass = jnp.sum(massb[...], axis=1, keepdims=True)
        colb[...] = jnp.broadcast_to(target / mass, colb.shape)

        def row_block(i, totals):
            at = pl.ds(pl.multiple_of(i * 8, 8), 8)
            col = colb[at, :]
            return tuple(total + w[at, t * LANES:(t + 1) * LANES] * col for t, total in enumerate(totals))

        totals = lax.fori_loop(
            0, mine // 8, row_block, tuple(jnp.zeros((8, LANES), jnp.float32) for _ in range(tiles)), unroll=8)
        total = jnp.concatenate([jnp.sum(part, axis=0, keepdims=True) for part in totals], axis=0)

        part_a[step] = total.astype(jnp.bfloat16)
        copies = []
        for j, (q, s) in enumerate(plane):
            copy = pltpu.make_async_remote_copy(
                src_ref=part_a.at[step], dst_ref=box_a.at[step, j], send_sem=asend.at[step, j],
                recv_sem=arecv.at[step, j], device_id=plane_dev(q, s), device_id_type=MESH)
            copy.start()
            copies.append(copy)
        for j, copy in reversed(list(enumerate(copies))):
            copy.wait_recv()
            total = total + box_a[step, j].astype(jnp.float32)
        sent.extend(copies)
        part_b[step] = total.astype(jnp.bfloat16)
        copies = []
        for e in reversed(range(1, depth)):
            copy = pltpu.make_async_remote_copy(
                src_ref=part_b.at[step], dst_ref=box_b.at[step, e], send_sem=bsend.at[step, e],
                recv_sem=brecv.at[step, e], device_id=z_dev(e), device_id_type=MESH)
            copy.start()
            copies.append(copy)
        for e, copy in zip(range(1, depth), reversed(copies)):
            copy.wait_recv()
            total = total + box_b[step, e].astype(jnp.float32)
        sent.extend(copies)
        row_scale = 1.0 / total

    scales = [jnp.broadcast_to(row_scale[t:t + 1, :], (16, LANES)) for t in range(tiles)]

    def block(i, carry):
        at = pl.ds(pl.multiple_of(i * 16, 16), 16)
        col = colb[at, :]
        mass = jnp.zeros((16, LANES), jnp.float32)
        for t in range(tiles):
            term = w[at, t * LANES:(t + 1) * LANES] * scales[t] * col
            mass = mass + term
            plan[at, t * LANES:(t + 1) * LANES] = term.astype(jnp.bfloat16)
        massb[at, :] = mass
        return carry

    lax.fori_loop(0, mine // 16, block, 0, unroll=4)
    massb[...] = jnp.broadcast_to(jnp.sum(massb[...], axis=1, keepdims=True), massb.shape)

    width = out.shape[1]
    results = []
    for q in (3, 1, 2, 0):
        peer = flip(r, q)
        cols = pl.ds(pl.multiple_of(peer * width, width), width)
        sums = jnp.dot(plan[...], v[:, cols], preferred_element_type=jnp.float32)
        mass = jnp.concatenate([massb[...]] * (width // LANES), axis=1)
        outbuf[q] = (0.5 * cent[:, cols].astype(jnp.float32) + 0.5 * sums / mass).astype(jnp.bfloat16)
        dst = out.at[pl.ds(pl.multiple_of(r * mine, mine), mine), :]
        if q:
            copy = pltpu.make_async_remote_copy(
                src_ref=outbuf.at[q], dst_ref=dst, send_sem=osend.at[q], recv_sem=orecv.at[q],
                device_id=(peer, c), device_id_type=MESH)
        else:
            copy = pltpu.make_async_copy(outbuf.at[q], dst, lsem.at[2])
        copy.start()
        results.append((q, copy))

    massrow[...] = jnp.transpose(massb[...], (1, 0))[:1, :]
    mdst = mass_out.at[r]
    mcopies = []
    for q in range(1, R):
        copy = pltpu.make_async_remote_copy(
            src_ref=massrow, dst_ref=mdst, send_sem=msend.at[q], recv_sem=mrecv.at[q],
            device_id=(flip(r, q), c), device_id_type=MESH)
        copy.start()
        mcopies.append(copy)
    local = pltpu.make_async_copy(massrow, mdst, lsem.at[3])
    local.start()

    for copy in sent:
        copy.wait_send()
    if passed:
        @pl.when(inner == 1)
        def _():
            for copy in passed:
                copy.wait_send()
    local.wait()
    for copy in mcopies:
        copy.wait()
    for q, copy in results:
        copy.wait()


def body(vectors, centroids, shards):
    rows, embed = vectors.shape
    batch = rows * R * shards
    held = centroids.shape[0]
    mine = held // R
    width = embed // R
    target = batch / (held * shards)
    depth = shards // 2
    tiles = batch // LANES
    f32, bf16 = jnp.float32, jnp.bfloat16
    dma = pltpu.SemaphoreType.DMA
    limit = 51 << 20
    updated, masses = pl.pallas_call(
        functools.partial(kernel, shards, target),
        out_shape=(jax.ShapeDtypeStruct((held, width), bf16), jax.ShapeDtypeStruct((R, 1, mine), f32)),
        in_specs=[pl.BlockSpec(memory_space=pltpu.VMEM), pl.BlockSpec(memory_space=pl.ANY)],
        out_specs=(pl.BlockSpec(memory_space=pl.ANY), pl.BlockSpec(memory_space=pl.ANY)),
        scratch_shapes=[
            pltpu.VMEM((batch, embed), bf16),
            pltpu.VMEM((mine, batch), f32),
            pltpu.VMEM((mine, batch), bf16),
            pltpu.VMEM((mine, embed), bf16),
            pltpu.VMEM((mine, LANES), f32),
            pltpu.VMEM((mine, LANES), f32),
            pltpu.VMEM((1, mine), f32),
            pltpu.VMEM((R, mine, width), bf16),
            pltpu.VMEM((ROUNDS, tiles, LANES), bf16),
            pltpu.VMEM((ROUNDS, tiles, LANES), bf16),
            pltpu.VMEM((ROUNDS, 2 * R - 1, tiles, LANES), bf16),
            pltpu.VMEM((ROUNDS, depth, tiles, LANES), bf16),
            dma((depth * 9,)), dma((4,)), dma((shards * R * 2,)),
            dma((ROUNDS, 2 * R)), dma((ROUNDS, 2 * R)),
            dma((ROUNDS, depth)), dma((ROUNDS, depth)),
            dma((R,)), dma((R,)), dma((R,)), dma((R,)), dma((4,)),
        ],
        compiler_params=pltpu.CompilerParams(
            collective_id=0, has_side_effects=True, vmem_limit_bytes=limit),
        cost_estimate=pl.CostEstimate(
            flops=4 * mine * batch * embed, bytes_accessed=2 * mine * embed * 4, transcendentals=mine * batch),
    )(vectors, centroids)
    return updated, masses.reshape(held)


def solution(mesh):
    from jax.sharding import PartitionSpec as P
    return jax.shard_map(
        functools.partial(body, shards=mesh.shape["cents"]),
        mesh=mesh,
        in_specs=(P(("rows", "cents"), None), P("cents", None)),
        out_specs=(P("cents", "rows"), P("cents")),
        check_vma=False,
    )
```

```python
import functools

import jax
import jax.numpy as jnp
from jax import lax
from jax.experimental import pallas as pl
from jax.experimental.pallas import tpu as pltpu

ROUNDS = 3
SHARP = 0.75
R = 4
LANES = 128
MESH = pl.DeviceIdType.MESH


def flip(a, d):
    out, bit = a, 1
    while bit <= d:
        if d & bit:
            out = out + bit - 2 * bit * lax.rem(lax.div(out, bit), 2)
        bit *= 2
    return out


def kernel(shards, target, vec, cent_hbm, out, mass_out, v, w, plan, cent, colb, massb, massrow, outbuf,
           part_a, part_b, box_a, box_b,
           gsend, psend, grecv, asend, arecv, bsend, brecv, osend, orecv, msend, mrecv, lsem):
    r, c = lax.axis_index("rows"), lax.axis_index("cents")
    z, k = lax.div(c, 2), lax.rem(c, 2)
    depth = shards // 2
    rows = vec.shape[0]
    half = rows // 2
    mine = cent.shape[0]
    batch = v.shape[0]
    chunk = R * rows
    tiles = batch // LANES

    plane = [(3, 1), (3, 0), (2, 1), (1, 1), (2, 0), (1, 0), (0, 1)]

    def plane_dev(q, s):
        return (flip(r, q), flip(c, s))

    def z_dev(e):
        return (r, flip(z, e) * 2 + k)

    barrier = pltpu.get_barrier_semaphore()
    for q, s in plane:
        pl.semaphore_signal(barrier, inc=1, device_id=plane_dev(q, s), device_id_type=MESH)
    for e in range(1, depth):
        pl.semaphore_signal(barrier, inc=1, device_id=z_dev(e), device_id_type=MESH)
    cent_in = pltpu.make_async_copy(
        cent_hbm.at[pl.ds(pl.multiple_of(r * mine, mine), mine), :], cent, lsem.at[0])
    cent_in.start()
    pl.semaphore_wait(barrier, len(plane) + depth - 1)

    sent = []

    def piece(cc, rr, part):
        base = (cc * R + rr) * rows
        if part == 2:
            return v.at[pl.ds(pl.multiple_of(base, rows), rows), :]
        return v.at[pl.ds(pl.multiple_of(base + part * half, half), half), :]

    def gsem(cc, rr, part):
        return grecv.at[(cc * R + rr) * 2 + (0 if part == 2 else part)]

    def send(cc, rr, part, dev, src=None):
        copy = pltpu.make_async_remote_copy(
            src_ref=piece(cc, rr, part) if src is None else src,
            dst_ref=piece(cc, rr, part),
            send_sem=gsend.at[len(sent)],
            recv_sem=gsem(cc, rr, part),
            device_id=dev, device_id_type=MESH)
        copy.start()
        sent.append(copy)

    def arrive(cc, rr, part):
        ref = piece(cc, rr, part)
        pltpu.make_async_remote_copy(
            src_ref=ref, dst_ref=ref, send_sem=gsend.at[0], recv_sem=gsem(cc, rr, part),
            device_id=plane_dev(0, 1), device_id_type=MESH).wait_recv()

    east, north, other = plane_dev(1, 0), plane_dev(2, 0), plane_dev(0, 1)
    rx, ry, rd = flip(r, 1), flip(r, 2), flip(r, 3)

    line = depth == 4
    inner = lax.rem(lax.div(z + 1, 2), 2)

    def source(d):
        if line and d >= 2:
            return inner * flip(z, 5 - d) + (1 - inner) * flip(z, d)
        return flip(z, d)

    passed = []

    def pass_on(cc, e, part, src=None):
        n = len(passed)
        copy = pltpu.make_async_remote_copy(
            src_ref=piece(cc, r, part) if src is None else src,
            dst_ref=piece(cc, r, part),
            send_sem=psend.at[n], recv_sem=gsem(cc, r, part),
            device_id=z_dev(e), device_id_type=MESH)
        passed.append(copy)

        @pl.when(inner == 1)
        def _():
            copy.start()

    halves = [vec.at[pl.ds(0, half), :], vec.at[pl.ds(half, half), :]]

    def column(d):
        cc = source(d) * 2 + k
        for part, first in ((0, east), (1, north)):
            src = None if d else halves[part]
            if d:
                arrive(cc, r, part)
                if line:
                    pass_on(cc, 3 if d == 1 else 1, part)
            else:
                if depth > 1:
                    send(cc, r, part, z_dev(1), src)
                if line:
                    pass_on(cc, 3, part, src)
            send(cc, r, part, first, src)
        for part, second in ((1, east), (0, north)):
            send(cc, r, part, second, None if d else halves[part])
        send(cc, r, 2, other, None if d else vec)

    def relay(d):
        cc = source(d) * 2 + k
        arrive(cc, rx, 0)
        send(cc, rx, 0, north)
        arrive(cc, ry, 1)
        send(cc, ry, 1, east)
        arrive(cc, rx, 1)
        send(cc, rx, 2, other)
        arrive(cc, ry, 0)
        send(cc, ry, 2, other)

    def corner(d):
        cc = source(d) * 2 + k
        arrive(cc, rd, 0)
        arrive(cc, rd, 1)
        send(cc, rd, 2, other)

    def weigh(cc):
        start = pl.multiple_of(cc * chunk, chunk)
        logits = lax.dot_general(
            cent[...], v[pl.ds(start, chunk), :], (((1,), (1,)), ((), ())),
            preferred_element_type=jnp.float32)
        terms = jnp.exp(SHARP * logits)
        w[:, pl.ds(start, chunk)] = terms
        sums = terms[:, :LANES]
        for t in range(1, chunk // LANES):
            sums = sums + terms[:, t * LANES:(t + 1) * LANES]
        massb[...] += sums

    massb[...] = jnp.zeros_like(massb)
    own = pltpu.make_async_copy(vec, piece(c, r, 2), lsem.at[1])
    own.start()
    column(0)
    if not line:
        for e in range(2, depth):
            for part in range(2):
                send(c, r, part, z_dev(e), halves[part])
    own.wait()
    cent_in.wait()

    def partner(d):
        cc = source(d) * 2 + 1 - k
        for rr in range(R):
            arrive(cc, rr, 2)
        weigh(cc)

    if depth > 1:
        column(1)
    relay(0)
    for d in range(depth):
        if d + 2 < depth:
            column(d + 2)
        if d + 1 < depth:
            relay(d + 1)
        if d:
            partner(d - 1)
        corner(d)
        weigh(source(d) * 2 + k)
    partner(depth - 1)

    for step in range(ROUNDS):
        if step:
            scales = [jnp.broadcast_to(row_scale[t:t + 1, :], (8, LANES)) for t in range(tiles)]

            def col_block(i, carry):
                at = pl.ds(pl.multiple_of(i * 8, 8), 8)
                sums = [w[at, t * LANES:(t + 1) * LANES] * scales[t] for t in range(tiles)]
                while len(sums) > 1:
                    sums = [a + b for a, b in zip(sums[::2], sums[1::2])] + ([sums[-1]] if len(sums) % 2 else [])
                massb[at, :] = sums[0]
                return carry

            lax.fori_loop(0, mine // 8, col_block, 0, unroll=8)
        mass = jnp.sum(massb[...], axis=1, keepdims=True)
        colb[...] = jnp.broadcast_to(target / mass, colb.shape)

        def row_block(i, totals):
            at = pl.ds(pl.multiple_of(i * 8, 8), 8)
            col = colb[at, :]
            return tuple(total + w[at, t * LANES:(t + 1) * LANES] * col for t, total in enumerate(totals))

        totals = lax.fori_loop(
            0, mine // 8, row_block, tuple(jnp.zeros((8, LANES), jnp.float32) for _ in range(tiles)), unroll=8)
        total = jnp.concatenate([jnp.sum(part, axis=0, keepdims=True) for part in totals], axis=0)

        part_a[step] = total.astype(jnp.bfloat16)
        copies = []
        for j, (q, s) in enumerate(plane):
            copy = pltpu.make_async_remote_copy(
                src_ref=part_a.at[step], dst_ref=box_a.at[step, j], send_sem=asend.at[step, j],
                recv_sem=arecv.at[step, j], device_id=plane_dev(q, s), device_id_type=MESH)
            copy.start()
            copies.append(copy)
        for j, copy in reversed(list(enumerate(copies))):
            copy.wait_recv()
            total = total + box_a[step, j].astype(jnp.float32)
        sent.extend(copies)
        part_b[step] = total.astype(jnp.bfloat16)
        copies = []
        for e in reversed(range(1, depth)):
            copy = pltpu.make_async_remote_copy(
                src_ref=part_b.at[step], dst_ref=box_b.at[step, e], send_sem=bsend.at[step, e],
                recv_sem=brecv.at[step, e], device_id=z_dev(e), device_id_type=MESH)
            copy.start()
            copies.append(copy)
        for e, copy in zip(range(1, depth), reversed(copies)):
            copy.wait_recv()
            total = total + box_b[step, e].astype(jnp.float32)
        sent.extend(copies)
        row_scale = 1.0 / total

    scales = [jnp.broadcast_to(row_scale[t:t + 1, :], (16, LANES)) for t in range(tiles)]

    def block(i, carry):
        at = pl.ds(pl.multiple_of(i * 16, 16), 16)
        col = colb[at, :]
        mass = jnp.zeros((16, LANES), jnp.float32)
        for t in range(tiles):
            term = w[at, t * LANES:(t + 1) * LANES] * scales[t] * col
            mass = mass + term
            plan[at, t * LANES:(t + 1) * LANES] = term.astype(jnp.bfloat16)
        massb[at, :] = mass
        return carry

    lax.fori_loop(0, mine // 16, block, 0, unroll=4)
    massb[...] = jnp.broadcast_to(jnp.sum(massb[...], axis=1, keepdims=True), massb.shape)

    width = out.shape[1]
    results = []
    for q in (3, 1, 2, 0):
        peer = flip(r, q)
        cols = pl.ds(pl.multiple_of(peer * width, width), width)
        sums = jnp.dot(plan[...], v[:, cols], preferred_element_type=jnp.float32)
        mass = jnp.concatenate([massb[...]] * (width // LANES), axis=1)
        outbuf[q] = (0.5 * cent[:, cols].astype(jnp.float32) + 0.5 * sums / mass).astype(jnp.bfloat16)
        dst = out.at[pl.ds(pl.multiple_of(r * mine, mine), mine), :]
        if q:
            copy = pltpu.make_async_remote_copy(
                src_ref=outbuf.at[q], dst_ref=dst, send_sem=osend.at[q], recv_sem=orecv.at[q],
                device_id=(peer, c), device_id_type=MESH)
        else:
            copy = pltpu.make_async_copy(outbuf.at[q], dst, lsem.at[2])
        copy.start()
        results.append((q, copy))

    massrow[...] = jnp.transpose(massb[...], (1, 0))[:1, :]
    mdst = mass_out.at[r]
    mcopies = []
    for q in range(1, R):
        copy = pltpu.make_async_remote_copy(
            src_ref=massrow, dst_ref=mdst, send_sem=msend.at[q], recv_sem=mrecv.at[q],
            device_id=(flip(r, q), c), device_id_type=MESH)
        copy.start()
        mcopies.append(copy)
    local = pltpu.make_async_copy(massrow, mdst, lsem.at[3])
    local.start()

    for copy in sent:
        copy.wait_send()
    if passed:
        @pl.when(inner == 1)
        def _():
            for copy in passed:
                copy.wait_send()
    local.wait()
    for copy in mcopies:
        copy.wait()
    for q, copy in results:
        copy.wait()


def body(vectors, centroids, shards):
    rows, embed = vectors.shape
    batch = rows * R * shards
    held = centroids.shape[0]
    mine = held // R
    width = embed // R
    target = batch / (held * shards)
    depth = shards // 2
    tiles = batch // LANES
    f32, bf16 = jnp.float32, jnp.bfloat16
    dma = pltpu.SemaphoreType.DMA
    limit = 51 << 20
    updated, masses = pl.pallas_call(
        functools.partial(kernel, shards, target),
        out_shape=(jax.ShapeDtypeStruct((held, width), bf16), jax.ShapeDtypeStruct((R, 1, mine), f32)),
        in_specs=[pl.BlockSpec(memory_space=pltpu.VMEM), pl.BlockSpec(memory_space=pl.ANY)],
        out_specs=(pl.BlockSpec(memory_space=pl.ANY), pl.BlockSpec(memory_space=pl.ANY)),
        scratch_shapes=[
            pltpu.VMEM((batch, embed), bf16),
            pltpu.VMEM((mine, batch), f32),
            pltpu.VMEM((mine, batch), bf16),
            pltpu.VMEM((mine, embed), bf16),
            pltpu.VMEM((mine, LANES), f32),
            pltpu.VMEM((mine, LANES), f32),
            pltpu.VMEM((1, mine), f32),
            pltpu.VMEM((R, mine, width), bf16),
            pltpu.VMEM((ROUNDS, tiles, LANES), bf16),
            pltpu.VMEM((ROUNDS, tiles, LANES), bf16),
            pltpu.VMEM((ROUNDS, 2 * R - 1, tiles, LANES), bf16),
            pltpu.VMEM((ROUNDS, depth, tiles, LANES), bf16),
            dma((depth * 12,)), dma((8,)), dma((shards * R * 2,)),
            dma((ROUNDS, 2 * R)), dma((ROUNDS, 2 * R)),
            dma((ROUNDS, depth)), dma((ROUNDS, depth)),
            dma((R,)), dma((R,)), dma((R,)), dma((R,)), dma((4,)),
        ],
        compiler_params=pltpu.CompilerParams(
            collective_id=0, has_side_effects=True, vmem_limit_bytes=limit),
        cost_estimate=pl.CostEstimate(
            flops=4 * mine * batch * embed, bytes_accessed=2 * mine * embed * 4, transcendentals=mine * batch),
    )(vectors, centroids)
    return updated, masses.reshape(held)


def solution(mesh):
    from jax.sharding import PartitionSpec as P
    return jax.shard_map(
        functools.partial(body, shards=mesh.shape["cents"]),
        mesh=mesh,
        in_specs=(P(("rows", "cents"), None), P("cents", None)),
        out_specs=(P("cents", "rows"), P("cents")),
        check_vma=False,
    )
```

```python
import functools

import jax
import jax.numpy as jnp
from jax import lax
from jax.experimental import pallas as pl
from jax.experimental.pallas import tpu as pltpu

ROUNDS = 3
SHARP = 0.75
R = 4
LANES = 128
PIECES = 8
MESH = pl.DeviceIdType.MESH


def flip(a, d):
    out, bit = a, 1
    while bit <= d:
        if d & bit:
            out = out + bit - 2 * bit * lax.rem(lax.div(out, bit), 2)
        bit *= 2
    return out


def kernel(shards, target, vec, cent_hbm, out, mass_out, v, w, plan, cent, colb, massb, massrow, outbuf,
           part_a, part_b, box_a, box_b,
           gsend, psend, qrecv, grecv, asend, arecv, bsend, brecv, osend, orecv, msend, mrecv, lsem):
    r, c = lax.axis_index("rows"), lax.axis_index("cents")
    z, k = lax.div(c, 2), lax.rem(c, 2)
    depth = shards // 2
    rows = vec.shape[0]
    half = rows // 2
    mine = cent.shape[0]
    batch = v.shape[0]
    chunk = R * rows
    tiles = batch // LANES

    plane = [(3, 1), (3, 0), (2, 1), (1, 1), (2, 0), (1, 0), (0, 1)]

    def plane_dev(q, s):
        return (flip(r, q), flip(c, s))

    def z_dev(e):
        return (r, flip(z, e) * 2 + k)

    barrier = pltpu.get_barrier_semaphore()
    for q, s in plane:
        pl.semaphore_signal(barrier, inc=1, device_id=plane_dev(q, s), device_id_type=MESH)
    for e in range(1, depth):
        pl.semaphore_signal(barrier, inc=1, device_id=z_dev(e), device_id_type=MESH)
    cent_in = pltpu.make_async_copy(
        cent_hbm.at[pl.ds(pl.multiple_of(r * mine, mine), mine), :], cent, lsem.at[0])
    cent_in.start()
    pl.semaphore_wait(barrier, len(plane) + depth - 1)

    sent = []

    line = depth == 4
    embed = vec.shape[1]
    cut = embed - LANES if line else embed

    def piece(cc, rr, part, width):
        base = (cc * R + rr) * rows
        if part == 2:
            return v.at[pl.ds(pl.multiple_of(base, rows), rows), pl.ds(0, width)]
        return v.at[pl.ds(pl.multiple_of(base + part * half, half), half), pl.ds(0, width)]

    def gsem(cc, rr, part):
        return grecv.at[(cc * R + rr) * 2 + (0 if part == 2 else part)]

    def send(cc, rr, part, dev, width, src=None):
        copy = pltpu.make_async_remote_copy(
            src_ref=piece(cc, rr, part, width) if src is None else src,
            dst_ref=piece(cc, rr, part, width),
            send_sem=gsend.at[len(sent)],
            recv_sem=gsem(cc, rr, part),
            device_id=dev, device_id_type=MESH)
        copy.start()
        sent.append(copy)

    def arrive(cc, rr, part, width):
        ref = piece(cc, rr, part, width)
        pltpu.make_async_remote_copy(
            src_ref=ref, dst_ref=ref, send_sem=gsend.at[0], recv_sem=gsem(cc, rr, part),
            device_id=plane_dev(0, 1), device_id_type=MESH).wait_recv()

    east, north, other = plane_dev(1, 0), plane_dev(2, 0), plane_dev(0, 1)
    rx, ry, rd = flip(r, 1), flip(r, 2), flip(r, 3)

    inner = lax.rem(lax.div(z + 1, 2), 2)

    def source(d):
        if line and d >= 2:
            return inner * flip(z, 5 - d) + (1 - inner) * flip(z, d)
        return flip(z, d)

    passed = []

    def pass_on(cc, e, part, src=None):
        n = len(passed)
        copy = pltpu.make_async_remote_copy(
            src_ref=piece(cc, r, part, cut) if src is None else src,
            dst_ref=piece(cc, r, part, cut),
            send_sem=psend.at[n], recv_sem=gsem(cc, r, part),
            device_id=z_dev(e), device_id_type=MESH)
        passed.append(copy)

        @pl.when(inner == 1)
        def _():
            copy.start()

    halves = [vec.at[pl.ds(0, half), :], vec.at[pl.ds(half, half), :]]
    parts = [vec.at[pl.ds(0, half), pl.ds(0, cut)], vec.at[pl.ds(half, half), pl.ds(0, cut)]]

    def column(d):
        cc = source(d) * 2 + k
        width = cut if d else embed
        for part, first in ((0, east), (1, north)):
            src = None if d else halves[part]
            if d:
                arrive(cc, r, part, cut)
                if line:
                    pass_on(cc, 3 if d == 1 else 1, part)
            else:
                if depth > 1:
                    send(cc, r, part, z_dev(1), cut, parts[part])
                if line:
                    pass_on(cc, 3, part, parts[part])
            send(cc, r, part, first, width, src)
        for part, second in ((1, east), (0, north)):
            send(cc, r, part, second, width, None if d else halves[part])
        send(cc, r, 2, other, width, None if d else vec)

    def relay(d):
        cc = source(d) * 2 + k
        width = cut if d else embed
        arrive(cc, rx, 0, width)
        send(cc, rx, 0, north, width)
        arrive(cc, ry, 1, width)
        send(cc, ry, 1, east, width)
        arrive(cc, rx, 1, width)
        send(cc, rx, 2, other, width)
        arrive(cc, ry, 0, width)
        send(cc, ry, 2, other, width)

    def corner(d):
        cc = source(d) * 2 + k
        width = cut if d else embed
        arrive(cc, rd, 0, width)
        arrive(cc, rd, 1, width)
        send(cc, rd, 2, other, width)

    def strip_copy(cc, dev, sem):
        ref = v.at[pl.ds(pl.multiple_of(cc * chunk, chunk), chunk), pl.ds(cut, LANES)]
        return pltpu.make_async_remote_copy(
            src_ref=ref, dst_ref=ref, send_sem=sem, recv_sem=qrecv.at[cc],
            device_id=dev, device_id_type=MESH)

    def strip(d):
        cc = source(d) * 2 + k
        if d:
            strip_copy(cc, other, gsend.at[0]).wait_recv()
        on = strip_copy(cc, z_dev(1 if d > 1 else 3), psend.at[len(passed)])
        passed.append(on)

        @pl.when(inner == 1)
        def _():
            on.start()

        copy = strip_copy(cc, other if d else z_dev(1), gsend.at[len(sent)])
        copy.start()
        sent.append(copy)

    def weigh(cc):
        start = pl.multiple_of(cc * chunk, chunk)
        logits = lax.dot_general(
            cent[...], v[pl.ds(start, chunk), :], (((1,), (1,)), ((), ())),
            preferred_element_type=jnp.float32)
        terms = jnp.exp(SHARP * logits)
        w[:, pl.ds(start, chunk)] = terms
        sums = terms[:, :LANES]
        for t in range(1, chunk // LANES):
            sums = sums + terms[:, t * LANES:(t + 1) * LANES]
        massb[...] += sums

    massb[...] = jnp.zeros_like(massb)
    own = pltpu.make_async_copy(vec, piece(c, r, 2, embed), lsem.at[1])
    own.start()
    column(0)
    if not line:
        for e in range(2, depth):
            for part in range(2):
                send(c, r, part, z_dev(e), embed, halves[part])
    own.wait()
    cent_in.wait()

    def partner(d):
        cc = source(d) * 2 + 1 - k
        for rr in range(R):
            arrive(cc, rr, 2, cut if d else embed)
        if line and d:
            strip_copy(cc, other, gsend.at[0]).wait_recv()
        weigh(cc)

    if depth > 1:
        column(1)
    relay(0)
    for d in range(depth):
        if d + 2 < depth:
            column(d + 2)
        if d + 1 < depth:
            relay(d + 1)
        if d:
            partner(d - 1)
        corner(d)
        if line:
            strip(d)
        weigh(source(d) * 2 + k)
    partner(depth - 1)

    for step in range(ROUNDS):
        if step:
            scales = [jnp.broadcast_to(row_scale[t:t + 1, :], (8, LANES)) for t in range(tiles)]

            def col_block(i, carry):
                at = pl.ds(pl.multiple_of(i * 8, 8), 8)
                sums = [w[at, t * LANES:(t + 1) * LANES] * scales[t] for t in range(tiles)]
                while len(sums) > 1:
                    sums = [a + b for a, b in zip(sums[::2], sums[1::2])] + ([sums[-1]] if len(sums) % 2 else [])
                massb[at, :] = sums[0]
                return carry

            lax.fori_loop(0, mine // 8, col_block, 0, unroll=8)
        mass = jnp.sum(massb[...], axis=1, keepdims=True)
        colb[...] = jnp.broadcast_to(target / mass, colb.shape)

        def row_block(i, totals):
            at = pl.ds(pl.multiple_of(i * 8, 8), 8)
            col = colb[at, :]
            return tuple(total + w[at, t * LANES:(t + 1) * LANES] * col for t, total in enumerate(totals))

        totals = lax.fori_loop(
            0, mine // 8, row_block, tuple(jnp.zeros((8, LANES), jnp.float32) for _ in range(tiles)), unroll=8)
        total = jnp.concatenate([jnp.sum(part, axis=0, keepdims=True) for part in totals], axis=0)

        part_a[step] = total.astype(jnp.bfloat16)
        copies = []
        for j, (q, s) in enumerate(plane):
            copy = pltpu.make_async_remote_copy(
                src_ref=part_a.at[step], dst_ref=box_a.at[step, j], send_sem=asend.at[step, j],
                recv_sem=arecv.at[step, j], device_id=plane_dev(q, s), device_id_type=MESH)
            copy.start()
            copies.append(copy)
        for j, copy in reversed(list(enumerate(copies))):
            copy.wait_recv()
            total = total + box_a[step, j].astype(jnp.float32)
        sent.extend(copies)
        part_b[step] = total.astype(jnp.bfloat16)
        copies = []
        for e in reversed(range(1, depth)):
            copy = pltpu.make_async_remote_copy(
                src_ref=part_b.at[step], dst_ref=box_b.at[step, e], send_sem=bsend.at[step, e],
                recv_sem=brecv.at[step, e], device_id=z_dev(e), device_id_type=MESH)
            copy.start()
            copies.append(copy)
        for e, copy in zip(range(1, depth), reversed(copies)):
            copy.wait_recv()
            total = total + box_b[step, e].astype(jnp.float32)
        sent.extend(copies)
        row_scale = 1.0 / total

    scales = [jnp.broadcast_to(row_scale[t:t + 1, :], (16, LANES)) for t in range(tiles)]

    def block(i, carry):
        at = pl.ds(pl.multiple_of(i * 16, 16), 16)
        col = colb[at, :]
        mass = jnp.zeros((16, LANES), jnp.float32)
        for t in range(tiles):
            term = w[at, t * LANES:(t + 1) * LANES] * scales[t] * col
            mass = mass + term
            plan[at, t * LANES:(t + 1) * LANES] = term.astype(jnp.bfloat16)
        massb[at, :] = mass
        return carry

    lax.fori_loop(0, mine // 16, block, 0, unroll=4)
    massb[...] = jnp.broadcast_to(jnp.sum(massb[...], axis=1, keepdims=True), massb.shape)

    width = out.shape[1]
    results = []
    for q in (3, 1, 2, 0):
        peer = flip(r, q)
        cols = pl.ds(pl.multiple_of(peer * width, width), width)
        sums = jnp.dot(plan[...], v[:, cols], preferred_element_type=jnp.float32)
        mass = jnp.concatenate([massb[...]] * (width // LANES), axis=1)
        outbuf[q] = (0.5 * cent[:, cols].astype(jnp.float32) + 0.5 * sums / mass).astype(jnp.bfloat16)
        dst = out.at[pl.ds(pl.multiple_of(r * mine, mine), mine), :]
        if q:
            copy = pltpu.make_async_remote_copy(
                src_ref=outbuf.at[q], dst_ref=dst, send_sem=osend.at[q], recv_sem=orecv.at[q],
                device_id=(peer, c), device_id_type=MESH)
        else:
            copy = pltpu.make_async_copy(outbuf.at[q], dst, lsem.at[2])
        copy.start()
        results.append((q, copy))

    massrow[...] = jnp.transpose(massb[...], (1, 0))[:1, :]
    mdst = mass_out.at[r]
    mcopies = []
    for q in range(1, R):
        copy = pltpu.make_async_remote_copy(
            src_ref=massrow, dst_ref=mdst, send_sem=msend.at[q], recv_sem=mrecv.at[q],
            device_id=(flip(r, q), c), device_id_type=MESH)
        copy.start()
        mcopies.append(copy)
    local = pltpu.make_async_copy(massrow, mdst, lsem.at[3])
    local.start()

    for copy in sent:
        copy.wait_send()
    if passed:
        @pl.when(inner == 1)
        def _():
            for copy in passed:
                copy.wait_send()
    local.wait()
    for copy in mcopies:
        copy.wait()
    for q, copy in results:
        copy.wait()


def finish(updated, masses, updated_out, masses_out, sem):
    step = updated.shape[0] // PIECES
    copies = [pltpu.make_async_copy(masses, masses_out, sem.at[PIECES])]
    for i in range(PIECES):
        at = pl.ds(i * step, step)
        copies.append(pltpu.make_async_copy(updated.at[at, :], updated_out.at[at, :], sem.at[i]))
    for copy in copies:
        copy.start()
    for copy in copies:
        copy.wait()


def body(vectors, centroids, shards):
    rows, embed = vectors.shape
    batch = rows * R * shards
    held = centroids.shape[0]
    mine = held // R
    width = embed // R
    target = batch / (held * shards)
    depth = shards // 2
    tiles = batch // LANES
    f32, bf16 = jnp.float32, jnp.bfloat16
    dma = pltpu.SemaphoreType.DMA
    limit = 56 << 20
    updated, masses = pl.pallas_call(
        functools.partial(kernel, shards, target),
        out_shape=(jax.ShapeDtypeStruct((held, width), bf16), jax.ShapeDtypeStruct((R, 1, mine), f32)),
        in_specs=[pl.BlockSpec(memory_space=pltpu.VMEM), pl.BlockSpec(memory_space=pl.ANY)],
        out_specs=(pl.BlockSpec(memory_space=pl.ANY), pl.BlockSpec(memory_space=pl.ANY)),
        scratch_shapes=[
            pltpu.VMEM((batch, embed), bf16),
            pltpu.VMEM((mine, batch), f32),
            pltpu.VMEM((mine, batch), bf16),
            pltpu.VMEM((mine, embed), bf16),
            pltpu.VMEM((mine, LANES), f32),
            pltpu.VMEM((mine, LANES), f32),
            pltpu.VMEM((1, mine), f32),
            pltpu.VMEM((R, mine, width), bf16),
            pltpu.VMEM((ROUNDS, tiles, LANES), bf16),
            pltpu.VMEM((ROUNDS, tiles, LANES), bf16),
            pltpu.VMEM((ROUNDS, 2 * R - 1, tiles, LANES), bf16),
            pltpu.VMEM((ROUNDS, depth, tiles, LANES), bf16),
            dma((depth * 12,)), dma((12,)), dma((shards,)), dma((shards * R * 2,)),
            dma((ROUNDS, 2 * R)), dma((ROUNDS, 2 * R)),
            dma((ROUNDS, depth)), dma((ROUNDS, depth)),
            dma((R,)), dma((R,)), dma((R,)), dma((R,)), dma((4,)),
        ],
        compiler_params=pltpu.CompilerParams(
            collective_id=0, has_side_effects=True, vmem_limit_bytes=limit),
        cost_estimate=pl.CostEstimate(
            flops=4 * mine * batch * embed, bytes_accessed=2 * mine * embed * 4, transcendentals=mine * batch),
    )(vectors, centroids)
    updated, masses = pl.pallas_call(
        finish,
        out_shape=(jax.ShapeDtypeStruct(updated.shape, bf16), jax.ShapeDtypeStruct(masses.shape, f32)),
        in_specs=[pl.BlockSpec(memory_space=pl.ANY)] * 2,
        out_specs=(pl.BlockSpec(memory_space=pl.ANY),) * 2,
        scratch_shapes=[dma((PIECES + 1,))],
        compiler_params=pltpu.CompilerParams(vmem_limit_bytes=limit),
        cost_estimate=pl.CostEstimate(flops=0, bytes_accessed=2 * held * width * 2, transcendentals=0),
    )(updated, masses)
    return updated, masses.reshape(held)


def solution(mesh):
    from jax.sharding import PartitionSpec as P
    return jax.shard_map(
        functools.partial(body, shards=mesh.shape["cents"]),
        mesh=mesh,
        in_specs=(P(("rows", "cents"), None), P("cents", None)),
        out_specs=(P("cents", "rows"), P("cents")),
        check_vma=False,
    )
```

```python
import functools

import jax
import jax.numpy as jnp
from jax import lax
from jax.experimental import pallas as pl
from jax.experimental.pallas import tpu as pltpu

ROUNDS = 3
SHARP = 0.75
R = 4
LANES = 128
PIECES = 8
MESH = pl.DeviceIdType.MESH


def flip(a, d):
    out, bit = a, 1
    while bit <= d:
        if d & bit:
            out = out + bit - 2 * bit * lax.rem(lax.div(out, bit), 2)
        bit *= 2
    return out


def kernel(shards, target, vec, cent_hbm, out, mass_out, v, w, plan, cent, colb, massb, massrow, outbuf,
           part_a, part_b, box_a, box_b,
           gsend, psend, qrecv, grecv, asend, arecv, bsend, brecv, osend, orecv, msend, mrecv, lsem):
    r, c = lax.axis_index("rows"), lax.axis_index("cents")
    z, k = lax.div(c, 2), lax.rem(c, 2)
    depth = shards // 2
    rows = vec.shape[0]
    half = rows // 2
    mine = cent.shape[0]
    batch = v.shape[0]
    chunk = R * rows
    tiles = batch // LANES

    plane = [(3, 1), (3, 0), (2, 1), (1, 1), (2, 0), (1, 0), (0, 1)]

    def plane_dev(q, s):
        return (flip(r, q), flip(c, s))

    def z_dev(e):
        return (r, flip(z, e) * 2 + k)

    barrier = pltpu.get_barrier_semaphore()
    for q, s in plane:
        pl.semaphore_signal(barrier, inc=1, device_id=plane_dev(q, s), device_id_type=MESH)
    for e in range(1, depth):
        pl.semaphore_signal(barrier, inc=1, device_id=z_dev(e), device_id_type=MESH)
    cent_in = pltpu.make_async_copy(
        cent_hbm.at[pl.ds(pl.multiple_of(r * mine, mine), mine), :], cent, lsem.at[0])
    cent_in.start()
    pl.semaphore_wait(barrier, len(plane) + depth - 1)

    sent = []

    line = depth == 4
    embed = vec.shape[1]
    cut = embed - LANES if line else embed

    def piece(cc, rr, part, width):
        base = (cc * R + rr) * rows
        if part == 2:
            return v.at[pl.ds(pl.multiple_of(base, rows), rows), pl.ds(0, width)]
        return v.at[pl.ds(pl.multiple_of(base + part * half, half), half), pl.ds(0, width)]

    def gsem(cc, rr, part):
        return grecv.at[(cc * R + rr) * 2 + (0 if part == 2 else part)]

    def send(cc, rr, part, dev, width, src=None):
        copy = pltpu.make_async_remote_copy(
            src_ref=piece(cc, rr, part, width) if src is None else src,
            dst_ref=piece(cc, rr, part, width),
            send_sem=gsend.at[len(sent)],
            recv_sem=gsem(cc, rr, part),
            device_id=dev, device_id_type=MESH)
        copy.start()
        sent.append(copy)

    def arrive(cc, rr, part, width):
        ref = piece(cc, rr, part, width)
        pltpu.make_async_remote_copy(
            src_ref=ref, dst_ref=ref, send_sem=gsend.at[0], recv_sem=gsem(cc, rr, part),
            device_id=plane_dev(0, 1), device_id_type=MESH).wait_recv()

    east, north, other = plane_dev(1, 0), plane_dev(2, 0), plane_dev(0, 1)
    rx, ry, rd = flip(r, 1), flip(r, 2), flip(r, 3)

    inner = lax.rem(lax.div(z + 1, 2), 2)

    def source(d):
        if line and d >= 2:
            return inner * flip(z, 5 - d) + (1 - inner) * flip(z, d)
        return flip(z, d)

    passed = []

    def pass_on(cc, e, part, src=None):
        n = len(passed)
        copy = pltpu.make_async_remote_copy(
            src_ref=piece(cc, r, part, cut) if src is None else src,
            dst_ref=piece(cc, r, part, cut),
            send_sem=psend.at[n], recv_sem=gsem(cc, r, part),
            device_id=z_dev(e), device_id_type=MESH)
        passed.append(copy)

        @pl.when(inner == 1)
        def _():
            copy.start()

    halves = [vec.at[pl.ds(0, half), :], vec.at[pl.ds(half, half), :]]
    parts = [vec.at[pl.ds(0, half), pl.ds(0, cut)], vec.at[pl.ds(half, half), pl.ds(0, cut)]]

    def column(d):
        cc = source(d) * 2 + k
        width = cut if d else embed
        for part, first in ((0, east), (1, north)):
            src = None if d else halves[part]
            if d:
                arrive(cc, r, part, cut)
                if line:
                    pass_on(cc, 3 if d == 1 else 1, part)
            else:
                if depth > 1:
                    send(cc, r, part, z_dev(1), cut, parts[part])
                if line:
                    pass_on(cc, 3, part, parts[part])
            send(cc, r, part, first, width, src)
        for part, second in ((1, east), (0, north)):
            send(cc, r, part, second, width, None if d else halves[part])
        send(cc, r, 2, other, width, None if d else vec)

    def relay(d):
        cc = source(d) * 2 + k
        width = cut if d else embed
        arrive(cc, rx, 0, width)
        send(cc, rx, 0, north, width)
        arrive(cc, ry, 1, width)
        send(cc, ry, 1, east, width)
        arrive(cc, rx, 1, width)
        send(cc, rx, 2, other, width)
        arrive(cc, ry, 0, width)
        send(cc, ry, 2, other, width)

    def corner(d):
        cc = source(d) * 2 + k
        width = cut if d else embed
        arrive(cc, rd, 0, width)
        arrive(cc, rd, 1, width)
        send(cc, rd, 2, other, width)

    def strip_copy(cc, dev, sem):
        ref = v.at[pl.ds(pl.multiple_of(cc * chunk, chunk), chunk), pl.ds(cut, LANES)]
        return pltpu.make_async_remote_copy(
            src_ref=ref, dst_ref=ref, send_sem=sem, recv_sem=qrecv.at[cc],
            device_id=dev, device_id_type=MESH)

    def strip(d):
        cc = source(d) * 2 + k
        if d:
            strip_copy(cc, other, gsend.at[0]).wait_recv()
        on = strip_copy(cc, z_dev(1 if d > 1 else 3), psend.at[len(passed)])
        passed.append(on)

        @pl.when(inner == 1)
        def _():
            on.start()

        copy = strip_copy(cc, other if d else z_dev(1), gsend.at[len(sent)])
        copy.start()
        sent.append(copy)

    def weigh(cc):
        start = pl.multiple_of(cc * chunk, chunk)
        logits = lax.dot_general(
            cent[...], v[pl.ds(start, chunk), :], (((1,), (1,)), ((), ())),
            preferred_element_type=jnp.float32)
        terms = jnp.exp(SHARP * logits)
        w[:, pl.ds(start, chunk)] = terms
        sums = terms[:, :LANES]
        for t in range(1, chunk // LANES):
            sums = sums + terms[:, t * LANES:(t + 1) * LANES]
        massb[...] += sums

    massb[...] = jnp.zeros_like(massb)
    own = pltpu.make_async_copy(vec, piece(c, r, 2, embed), lsem.at[1])
    own.start()
    column(0)
    if not line:
        for e in range(2, depth):
            for part in range(2):
                send(c, r, part, z_dev(e), embed, halves[part])
    own.wait()
    cent_in.wait()

    def partner(d):
        cc = source(d) * 2 + 1 - k
        for rr in range(R):
            arrive(cc, rr, 2, cut if d else embed)
        if line and d:
            strip_copy(cc, other, gsend.at[0]).wait_recv()
        weigh(cc)

    if depth > 1:
        column(1)
    relay(0)
    for d in range(depth):
        if d + 2 < depth:
            column(d + 2)
        if d + 1 < depth:
            relay(d + 1)
        if d:
            partner(d - 1)
        corner(d)
        if line:
            strip(d)
        weigh(source(d) * 2 + k)
    partner(depth - 1)

    for step in range(ROUNDS):
        if step:
            scales = [jnp.broadcast_to(row_scale[t:t + 1, :], (8, LANES)) for t in range(tiles)]

            def col_block(i, carry):
                at = pl.ds(pl.multiple_of(i * 8, 8), 8)
                sums = [w[at, t * LANES:(t + 1) * LANES] * scales[t] for t in range(tiles)]
                while len(sums) > 1:
                    sums = [a + b for a, b in zip(sums[::2], sums[1::2])] + ([sums[-1]] if len(sums) % 2 else [])
                massb[at, :] = sums[0]
                return carry

            lax.fori_loop(0, mine // 8, col_block, 0, unroll=8)
        mass = jnp.sum(massb[...], axis=1, keepdims=True)
        colb[...] = jnp.broadcast_to(target / mass, colb.shape)

        def row_block(i, totals):
            at = pl.ds(pl.multiple_of(i * 8, 8), 8)
            col = colb[at, :]
            return tuple(total + w[at, t * LANES:(t + 1) * LANES] * col for t, total in enumerate(totals))

        totals = lax.fori_loop(
            0, mine // 8, row_block, tuple(jnp.zeros((8, LANES), jnp.float32) for _ in range(tiles)), unroll=8)
        total = jnp.concatenate([jnp.sum(part, axis=0, keepdims=True) for part in totals], axis=0)

        part_a[step] = total.astype(jnp.bfloat16)
        copies = []
        for j, (q, s) in enumerate(plane):
            copy = pltpu.make_async_remote_copy(
                src_ref=part_a.at[step], dst_ref=box_a.at[step, j], send_sem=asend.at[step, j],
                recv_sem=arecv.at[step, j], device_id=plane_dev(q, s), device_id_type=MESH)
            copy.start()
            copies.append(copy)
        for j, copy in reversed(list(enumerate(copies))):
            copy.wait_recv()
            total = total + box_a[step, j].astype(jnp.float32)
        sent.extend(copies)
        part_b[step] = total.astype(jnp.bfloat16)
        copies = []
        for e in reversed(range(1, depth)):
            copy = pltpu.make_async_remote_copy(
                src_ref=part_b.at[step], dst_ref=box_b.at[step, e], send_sem=bsend.at[step, e],
                recv_sem=brecv.at[step, e], device_id=z_dev(e), device_id_type=MESH)
            copy.start()
            copies.append(copy)
        for e, copy in zip(range(1, depth), reversed(copies)):
            copy.wait_recv()
            total = total + box_b[step, e].astype(jnp.float32)
        sent.extend(copies)
        row_scale = 1.0 / total

    scales = [jnp.broadcast_to(row_scale[t:t + 1, :], (16, LANES)) for t in range(tiles)]

    def block(i, carry):
        at = pl.ds(pl.multiple_of(i * 16, 16), 16)
        col = colb[at, :]
        mass = jnp.zeros((16, LANES), jnp.float32)
        for t in range(tiles):
            term = w[at, t * LANES:(t + 1) * LANES] * scales[t] * col
            mass = mass + term
            plan[at, t * LANES:(t + 1) * LANES] = term.astype(jnp.bfloat16)
        massb[at, :] = mass
        return carry

    lax.fori_loop(0, mine // 16, block, 0, unroll=4)
    massb[...] = jnp.broadcast_to(jnp.sum(massb[...], axis=1, keepdims=True), massb.shape)

    width = out.shape[1]
    results = []
    for q in (3, 1, 2, 0):
        peer = flip(r, q)
        cols = pl.ds(pl.multiple_of(peer * width, width), width)
        sums = jnp.dot(plan[...], v[:, cols], preferred_element_type=jnp.float32)
        mass = jnp.concatenate([massb[...]] * (width // LANES), axis=1)
        outbuf[q] = (0.5 * cent[:, cols].astype(jnp.float32) + 0.5 * sums / mass).astype(jnp.bfloat16)
        dst = out.at[pl.ds(pl.multiple_of(r * mine, mine), mine), :]
        if q:
            copy = pltpu.make_async_remote_copy(
                src_ref=outbuf.at[q], dst_ref=dst, send_sem=osend.at[q], recv_sem=orecv.at[q],
                device_id=(peer, c), device_id_type=MESH)
        else:
            copy = pltpu.make_async_copy(outbuf.at[q], dst, lsem.at[2])
        copy.start()
        results.append((q, copy))

    massrow[...] = jnp.transpose(massb[...], (1, 0))[:1, :]
    mdst = mass_out.at[r]
    mcopies = []
    for q in range(1, R):
        copy = pltpu.make_async_remote_copy(
            src_ref=massrow, dst_ref=mdst, send_sem=msend.at[q], recv_sem=mrecv.at[q],
            device_id=(flip(r, q), c), device_id_type=MESH)
        copy.start()
        mcopies.append(copy)
    local = pltpu.make_async_copy(massrow, mdst, lsem.at[3])
    local.start()

    for copy in sent:
        copy.wait_send()
    if passed:
        @pl.when(inner == 1)
        def _():
            for copy in passed:
                copy.wait_send()
    local.wait()
    for copy in mcopies:
        copy.wait()
    for q, copy in results:
        copy.wait()


def finish(updated, masses, updated_out, masses_out, sem):
    step = updated.shape[0] // PIECES
    copies = [pltpu.make_async_copy(masses, masses_out, sem.at[PIECES])]
    for i in range(PIECES):
        at = pl.ds(i * step, step)
        copies.append(pltpu.make_async_copy(updated.at[at, :], updated_out.at[at, :], sem.at[i]))
    for copy in copies:
        copy.start()
    for copy in copies:
        copy.wait()


def body(vectors, centroids, shards):
    rows, embed = vectors.shape
    batch = rows * R * shards
    held = centroids.shape[0]
    mine = held // R
    width = embed // R
    target = batch / (held * shards)
    depth = shards // 2
    tiles = batch // LANES
    f32, bf16 = jnp.float32, jnp.bfloat16
    dma = pltpu.SemaphoreType.DMA
    limit = 51 << 20
    updated, masses = pl.pallas_call(
        functools.partial(kernel, shards, target),
        out_shape=(jax.ShapeDtypeStruct((held, width), bf16), jax.ShapeDtypeStruct((R, 1, mine), f32)),
        in_specs=[pl.BlockSpec(memory_space=pltpu.VMEM), pl.BlockSpec(memory_space=pl.ANY)],
        out_specs=(pl.BlockSpec(memory_space=pl.ANY), pl.BlockSpec(memory_space=pl.ANY)),
        scratch_shapes=[
            pltpu.VMEM((batch, embed), bf16),
            pltpu.VMEM((mine, batch), f32),
            pltpu.VMEM((mine, batch), bf16),
            pltpu.VMEM((mine, embed), bf16),
            pltpu.VMEM((mine, LANES), f32),
            pltpu.VMEM((mine, LANES), f32),
            pltpu.VMEM((1, mine), f32),
            pltpu.VMEM((R, mine, width), bf16),
            pltpu.VMEM((ROUNDS, tiles, LANES), bf16),
            pltpu.VMEM((ROUNDS, tiles, LANES), bf16),
            pltpu.VMEM((ROUNDS, 2 * R - 1, tiles, LANES), bf16),
            pltpu.VMEM((ROUNDS, depth, tiles, LANES), bf16),
            dma((depth * 12,)), dma((12,)), dma((shards,)), dma((shards * R * 2,)),
            dma((ROUNDS, 2 * R)), dma((ROUNDS, 2 * R)),
            dma((ROUNDS, depth)), dma((ROUNDS, depth)),
            dma((R,)), dma((R,)), dma((R,)), dma((R,)), dma((4,)),
        ],
        compiler_params=pltpu.CompilerParams(
            collective_id=0, has_side_effects=True, vmem_limit_bytes=limit),
        cost_estimate=pl.CostEstimate(
            flops=4 * mine * batch * embed, bytes_accessed=2 * mine * embed * 4, transcendentals=mine * batch),
    )(vectors, centroids)
    updated, masses = pl.pallas_call(
        finish,
        out_shape=(jax.ShapeDtypeStruct(updated.shape, bf16), jax.ShapeDtypeStruct(masses.shape, f32)),
        in_specs=[pl.BlockSpec(memory_space=pl.ANY)] * 2,
        out_specs=(pl.BlockSpec(memory_space=pl.ANY),) * 2,
        scratch_shapes=[dma((PIECES + 1,))],
        compiler_params=pltpu.CompilerParams(vmem_limit_bytes=2 << 20),
        cost_estimate=pl.CostEstimate(flops=0, bytes_accessed=2 * held * width * 2, transcendentals=0),
    )(updated, masses)
    return updated, masses.reshape(held)


def solution(mesh):
    from jax.sharding import PartitionSpec as P
    return jax.shard_map(
        functools.partial(body, shards=mesh.shape["cents"]),
        mesh=mesh,
        in_specs=(P(("rows", "cents"), None), P("cents", None)),
        out_specs=(P("cents", "rows"), P("cents")),
        check_vma=False,
    )
```

```python
import functools

import jax
import jax.numpy as jnp
from jax import lax
from jax.experimental import pallas as pl
from jax.experimental.pallas import tpu as pltpu

ROUNDS = 3
SHARP = 0.75
R = 4
LANES = 128
PIECES = 2
MESH = pl.DeviceIdType.MESH


def flip(a, d):
    out, bit = a, 1
    while bit <= d:
        if d & bit:
            out = out + bit - 2 * bit * lax.rem(lax.div(out, bit), 2)
        bit *= 2
    return out


def kernel(shards, target, vec, cent_hbm, out, mass_out, v, w, plan, cent, colb, massb, massrow, outbuf,
           part_a, part_b, box_a, box_b,
           gsend, psend, qrecv, grecv, asend, arecv, bsend, brecv, osend, orecv, msend, mrecv, lsem):
    r, c = lax.axis_index("rows"), lax.axis_index("cents")
    z, k = lax.div(c, 2), lax.rem(c, 2)
    depth = shards // 2
    rows = vec.shape[0]
    half = rows // 2
    mine = cent.shape[0]
    batch = v.shape[0]
    chunk = R * rows
    tiles = batch // LANES

    plane = [(3, 1), (3, 0), (2, 1), (1, 1), (2, 0), (1, 0), (0, 1)]

    def plane_dev(q, s):
        return (flip(r, q), flip(c, s))

    def z_dev(e):
        return (r, flip(z, e) * 2 + k)

    barrier = pltpu.get_barrier_semaphore()
    for q, s in plane:
        pl.semaphore_signal(barrier, inc=1, device_id=plane_dev(q, s), device_id_type=MESH)
    for e in range(1, depth):
        pl.semaphore_signal(barrier, inc=1, device_id=z_dev(e), device_id_type=MESH)
    cent_in = pltpu.make_async_copy(
        cent_hbm.at[pl.ds(pl.multiple_of(r * mine, mine), mine), :], cent, lsem.at[0])
    cent_in.start()
    pl.semaphore_wait(barrier, len(plane) + depth - 1)

    sent = []

    line = depth == 4
    embed = vec.shape[1]
    cut = embed - LANES if line else embed

    def piece(cc, rr, part, width):
        base = (cc * R + rr) * rows
        if part == 2:
            return v.at[pl.ds(pl.multiple_of(base, rows), rows), pl.ds(0, width)]
        return v.at[pl.ds(pl.multiple_of(base + part * half, half), half), pl.ds(0, width)]

    def gsem(cc, rr, part):
        return grecv.at[(cc * R + rr) * 2 + (0 if part == 2 else part)]

    def send(cc, rr, part, dev, width, src=None):
        copy = pltpu.make_async_remote_copy(
            src_ref=piece(cc, rr, part, width) if src is None else src,
            dst_ref=piece(cc, rr, part, width),
            send_sem=gsend.at[len(sent)],
            recv_sem=gsem(cc, rr, part),
            device_id=dev, device_id_type=MESH)
        copy.start()
        sent.append(copy)

    def arrive(cc, rr, part, width):
        ref = piece(cc, rr, part, width)
        pltpu.make_async_remote_copy(
            src_ref=ref, dst_ref=ref, send_sem=gsend.at[0], recv_sem=gsem(cc, rr, part),
            device_id=plane_dev(0, 1), device_id_type=MESH).wait_recv()

    east, north, other = plane_dev(1, 0), plane_dev(2, 0), plane_dev(0, 1)
    rx, ry, rd = flip(r, 1), flip(r, 2), flip(r, 3)

    inner = lax.rem(lax.div(z + 1, 2), 2)

    def source(d):
        if line and d >= 2:
            return inner * flip(z, 5 - d) + (1 - inner) * flip(z, d)
        return flip(z, d)

    passed = []

    def pass_on(cc, e, part, src=None):
        n = len(passed)
        copy = pltpu.make_async_remote_copy(
            src_ref=piece(cc, r, part, cut) if src is None else src,
            dst_ref=piece(cc, r, part, cut),
            send_sem=psend.at[n], recv_sem=gsem(cc, r, part),
            device_id=z_dev(e), device_id_type=MESH)
        passed.append(copy)

        @pl.when(inner == 1)
        def _():
            copy.start()

    halves = [vec.at[pl.ds(0, half), :], vec.at[pl.ds(half, half), :]]
    parts = [vec.at[pl.ds(0, half), pl.ds(0, cut)], vec.at[pl.ds(half, half), pl.ds(0, cut)]]

    def column(d):
        cc = source(d) * 2 + k
        width = cut if d else embed
        for part, first in ((0, east), (1, north)):
            src = None if d else halves[part]
            if d:
                arrive(cc, r, part, cut)
                if line:
                    pass_on(cc, 3 if d == 1 else 1, part)
            else:
                if depth > 1:
                    send(cc, r, part, z_dev(1), cut, parts[part])
                if line:
                    pass_on(cc, 3, part, parts[part])
            send(cc, r, part, first, width, src)
        for part, second in ((1, east), (0, north)):
            send(cc, r, part, second, width, None if d else halves[part])
        send(cc, r, 2, other, width, None if d else vec)

    def relay(d):
        cc = source(d) * 2 + k
        width = cut if d else embed
        arrive(cc, rx, 0, width)
        send(cc, rx, 0, north, width)
        arrive(cc, ry, 1, width)
        send(cc, ry, 1, east, width)
        arrive(cc, rx, 1, width)
        send(cc, rx, 2, other, width)
        arrive(cc, ry, 0, width)
        send(cc, ry, 2, other, width)

    def corner(d):
        cc = source(d) * 2 + k
        width = cut if d else embed
        arrive(cc, rd, 0, width)
        arrive(cc, rd, 1, width)
        send(cc, rd, 2, other, width)

    def strip_copy(cc, dev, sem):
        ref = v.at[pl.ds(pl.multiple_of(cc * chunk, chunk), chunk), pl.ds(cut, LANES)]
        return pltpu.make_async_remote_copy(
            src_ref=ref, dst_ref=ref, send_sem=sem, recv_sem=qrecv.at[cc],
            device_id=dev, device_id_type=MESH)

    def strip(d):
        cc = source(d) * 2 + k
        if d:
            strip_copy(cc, other, gsend.at[0]).wait_recv()
        on = strip_copy(cc, z_dev(1 if d > 1 else 3), psend.at[len(passed)])
        passed.append(on)

        @pl.when(inner == 1)
        def _():
            on.start()

        copy = strip_copy(cc, other if d else z_dev(1), gsend.at[len(sent)])
        copy.start()
        sent.append(copy)

    def weigh(cc):
        start = pl.multiple_of(cc * chunk, chunk)
        logits = lax.dot_general(
            cent[...], v[pl.ds(start, chunk), :], (((1,), (1,)), ((), ())),
            preferred_element_type=jnp.float32)
        terms = jnp.exp(SHARP * logits)
        w[:, pl.ds(start, chunk)] = terms
        sums = terms[:, :LANES]
        for t in range(1, chunk // LANES):
            sums = sums + terms[:, t * LANES:(t + 1) * LANES]
        massb[...] += sums

    massb[...] = jnp.zeros_like(massb)
    own = pltpu.make_async_copy(vec, piece(c, r, 2, embed), lsem.at[1])
    own.start()
    column(0)
    if not line:
        for e in range(2, depth):
            for part in range(2):
                send(c, r, part, z_dev(e), embed, halves[part])
    own.wait()
    cent_in.wait()

    def partner(d):
        cc = source(d) * 2 + 1 - k
        for rr in range(R):
            arrive(cc, rr, 2, cut if d else embed)
        if line and d:
            strip_copy(cc, other, gsend.at[0]).wait_recv()
        weigh(cc)

    if depth > 1:
        column(1)
    relay(0)
    for d in range(depth):
        if d + 2 < depth:
            column(d + 2)
        if d + 1 < depth:
            relay(d + 1)
        if d:
            partner(d - 1)
        corner(d)
        if line:
            strip(d)
        weigh(source(d) * 2 + k)
    partner(depth - 1)

    for step in range(ROUNDS):
        if step:
            scales = [jnp.broadcast_to(row_scale[t:t + 1, :], (8, LANES)) for t in range(tiles)]

            def col_block(i, carry):
                at = pl.ds(pl.multiple_of(i * 8, 8), 8)
                sums = [w[at, t * LANES:(t + 1) * LANES] * scales[t] for t in range(tiles)]
                while len(sums) > 1:
                    sums = [a + b for a, b in zip(sums[::2], sums[1::2])] + ([sums[-1]] if len(sums) % 2 else [])
                massb[at, :] = sums[0]
                return carry

            lax.fori_loop(0, mine // 8, col_block, 0, unroll=16)
        mass = jnp.sum(massb[...], axis=1, keepdims=True)
        colb[...] = jnp.broadcast_to(target / mass, colb.shape)

        def row_block(i, totals):
            at = pl.ds(pl.multiple_of(i * 8, 8), 8)
            col = colb[at, :]
            return tuple(total + w[at, t * LANES:(t + 1) * LANES] * col for t, total in enumerate(totals))

        totals = lax.fori_loop(
            0, mine // 8, row_block, tuple(jnp.zeros((8, LANES), jnp.float32) for _ in range(tiles)), unroll=16)
        total = jnp.concatenate([jnp.sum(part, axis=0, keepdims=True) for part in totals], axis=0)

        part_a[step] = total.astype(jnp.bfloat16)
        copies = []
        for j, (q, s) in enumerate(plane):
            copy = pltpu.make_async_remote_copy(
                src_ref=part_a.at[step], dst_ref=box_a.at[step, j], send_sem=asend.at[step, j],
                recv_sem=arecv.at[step, j], device_id=plane_dev(q, s), device_id_type=MESH)
            copy.start()
            copies.append(copy)
        for j, copy in reversed(list(enumerate(copies))):
            copy.wait_recv()
            total = total + box_a[step, j].astype(jnp.float32)
        sent.extend(copies)
        part_b[step] = total.astype(jnp.bfloat16)
        copies = []
        for e in reversed(range(1, depth)):
            copy = pltpu.make_async_remote_copy(
                src_ref=part_b.at[step], dst_ref=box_b.at[step, e], send_sem=bsend.at[step, e],
                recv_sem=brecv.at[step, e], device_id=z_dev(e), device_id_type=MESH)
            copy.start()
            copies.append(copy)
        for e, copy in zip(range(1, depth), reversed(copies)):
            copy.wait_recv()
            total = total + box_b[step, e].astype(jnp.float32)
        sent.extend(copies)
        row_scale = 1.0 / total

    scales = [jnp.broadcast_to(row_scale[t:t + 1, :], (16, LANES)) for t in range(tiles)]

    def block(i, carry):
        at = pl.ds(pl.multiple_of(i * 16, 16), 16)
        col = colb[at, :]
        mass = jnp.zeros((16, LANES), jnp.float32)
        for t in range(tiles):
            term = w[at, t * LANES:(t + 1) * LANES] * scales[t] * col
            mass = mass + term
            plan[at, t * LANES:(t + 1) * LANES] = term.astype(jnp.bfloat16)
        massb[at, :] = mass
        return carry

    lax.fori_loop(0, mine // 16, block, 0, unroll=4)
    massb[...] = jnp.broadcast_to(jnp.sum(massb[...], axis=1, keepdims=True), massb.shape)

    width = out.shape[1]
    results = []
    for q in (3, 1, 2, 0):
        peer = flip(r, q)
        cols = pl.ds(pl.multiple_of(peer * width, width), width)
        sums = jnp.dot(plan[...], v[:, cols], preferred_element_type=jnp.float32)
        mass = jnp.concatenate([massb[...]] * (width // LANES), axis=1)
        outbuf[q] = (0.5 * cent[:, cols].astype(jnp.float32) + 0.5 * sums / mass).astype(jnp.bfloat16)
        dst = out.at[pl.ds(pl.multiple_of(r * mine, mine), mine), :]
        if q:
            copy = pltpu.make_async_remote_copy(
                src_ref=outbuf.at[q], dst_ref=dst, send_sem=osend.at[q], recv_sem=orecv.at[q],
                device_id=(peer, c), device_id_type=MESH)
        else:
            copy = pltpu.make_async_copy(outbuf.at[q], dst, lsem.at[2])
        copy.start()
        results.append((q, copy))

    massrow[...] = jnp.transpose(massb[...], (1, 0))[:1, :]
    mdst = mass_out.at[r]
    mcopies = []
    for q in range(1, R):
        copy = pltpu.make_async_remote_copy(
            src_ref=massrow, dst_ref=mdst, send_sem=msend.at[q], recv_sem=mrecv.at[q],
            device_id=(flip(r, q), c), device_id_type=MESH)
        copy.start()
        mcopies.append(copy)
    local = pltpu.make_async_copy(massrow, mdst, lsem.at[3])
    local.start()

    for copy in sent:
        copy.wait_send()
    if passed:
        @pl.when(inner == 1)
        def _():
            for copy in passed:
                copy.wait_send()
    local.wait()
    for copy in mcopies:
        copy.wait()
    for q, copy in results:
        copy.wait()


def finish(updated, masses, updated_out, masses_out, sem):
    step = updated.shape[0] // PIECES
    copies = [pltpu.make_async_copy(masses, masses_out, sem.at[PIECES])]
    for i in range(PIECES):
        at = pl.ds(i * step, step)
        copies.append(pltpu.make_async_copy(updated.at[at, :], updated_out.at[at, :], sem.at[i]))
    for copy in copies:
        copy.start()
    for copy in copies:
        copy.wait()


def body(vectors, centroids, shards):
    rows, embed = vectors.shape
    batch = rows * R * shards
    held = centroids.shape[0]
    mine = held // R
    width = embed // R
    target = batch / (held * shards)
    depth = shards // 2
    tiles = batch // LANES
    f32, bf16 = jnp.float32, jnp.bfloat16
    dma = pltpu.SemaphoreType.DMA
    limit = 51 << 20
    updated, masses = pl.pallas_call(
        functools.partial(kernel, shards, target),
        out_shape=(jax.ShapeDtypeStruct((held, width), bf16), jax.ShapeDtypeStruct((R, 1, mine), f32)),
        in_specs=[pl.BlockSpec(memory_space=pltpu.VMEM), pl.BlockSpec(memory_space=pl.ANY)],
        out_specs=(pl.BlockSpec(memory_space=pl.ANY), pl.BlockSpec(memory_space=pl.ANY)),
        scratch_shapes=[
            pltpu.VMEM((batch, embed), bf16),
            pltpu.VMEM((mine, batch), f32),
            pltpu.VMEM((mine, batch), bf16),
            pltpu.VMEM((mine, embed), bf16),
            pltpu.VMEM((mine, LANES), f32),
            pltpu.VMEM((mine, LANES), f32),
            pltpu.VMEM((1, mine), f32),
            pltpu.VMEM((R, mine, width), bf16),
            pltpu.VMEM((ROUNDS, tiles, LANES), bf16),
            pltpu.VMEM((ROUNDS, tiles, LANES), bf16),
            pltpu.VMEM((ROUNDS, 2 * R - 1, tiles, LANES), bf16),
            pltpu.VMEM((ROUNDS, depth, tiles, LANES), bf16),
            dma((depth * 12,)), dma((12,)), dma((shards,)), dma((shards * R * 2,)),
            dma((ROUNDS, 2 * R)), dma((ROUNDS, 2 * R)),
            dma((ROUNDS, depth)), dma((ROUNDS, depth)),
            dma((R,)), dma((R,)), dma((R,)), dma((R,)), dma((4,)),
        ],
        compiler_params=pltpu.CompilerParams(
            collective_id=0, has_side_effects=True, vmem_limit_bytes=limit),
        cost_estimate=pl.CostEstimate(
            flops=4 * mine * batch * embed, bytes_accessed=2 * mine * embed * 4, transcendentals=mine * batch),
    )(vectors, centroids)
    updated, masses = pl.pallas_call(
        finish,
        out_shape=(jax.ShapeDtypeStruct(updated.shape, bf16), jax.ShapeDtypeStruct(masses.shape, f32)),
        in_specs=[pl.BlockSpec(memory_space=pl.ANY)] * 2,
        out_specs=(pl.BlockSpec(memory_space=pl.ANY),) * 2,
        scratch_shapes=[dma((PIECES + 1,))],
        compiler_params=pltpu.CompilerParams(vmem_limit_bytes=2 << 20),
        cost_estimate=pl.CostEstimate(flops=0, bytes_accessed=2 * held * width * 2, transcendentals=0),
    )(updated, masses)
    return updated, masses.reshape(held)


def solution(mesh):
    from jax.sharding import PartitionSpec as P
    return jax.shard_map(
        functools.partial(body, shards=mesh.shape["cents"]),
        mesh=mesh,
        in_specs=(P(("rows", "cents"), None), P("cents", None)),
        out_specs=(P("cents", "rows"), P("cents")),
        check_vma=False,
    )
```
